256 devices in a mesh: leaf: 64 (over z, y, core), sub: 4 (over x).
Axes of the slice: x: 4, y: 4, z: 8, core: 2. Of those that a mesh axis runs over, the one named last changes fastest.
Arguments:
- points: float32 [3, 1048576], P(None, ('leaf', 'sub')), may hold values from 0 to 2048, as said below
- vectors: float32 [32, 1048576], P(None, ('leaf', 'sub')), may hold values from -6 to 6
- counts: int32 [2048, 8], P(('leaf', 'sub')), may hold values from 1 to 64, 384 in all within a row
Outputs:
- product: float32 [32, 1048576], P(None, ('leaf', 'sub'))
The draws below stay inside these ranges and needn't reach their ends.
Inputs may be any that keep to these rules, and one draw needn't show every extreme that they name: `points`: rows 0, 1, 2 are x, y, z. The slots of leaf l = 8 s + 4 cz + 2 cy + cx lie in its cell: x in [cx / 2, (cx + 1) / 2], y in [cy / 2, (cy + 1) / 2], z in [s + cz / 2, s + (cz + 1) / 2]. Leaf 8 s + c holds its points in its first counts[s, c] slots; later slots are empty. Each row sums to 384 and holds 64 at least once.
All inputs are finite; a program needn't handle non-finite values.
Results may differ from the reference program's by a relative error of at most 0.0003.
Values sent between devices are 32-bit elements; how exact they have to be, the bound alone decides.
No kernel may reach another device: no remote copies, remote signals or barrier semaphores. Data moves between devices by JAX's collectives and lax.ppermute only.
A program may use at most 128 MiB of HBM per device.

```python
import math
import jax
import jax.numpy as jnp
import numpy as np
from jax import lax

LEAF_PTS = 64
ORDER = 4
RANK = 64
VECS = 32
NSLAB = 2048
LEVELS = 10
NPTS = 1048576


def draw_points(key, part):
    leaf_count = NPTS // LEAF_PTS
    samples = jax.random.uniform(key, (3, leaf_count, LEAF_PTS), jnp.float32)
    leaves = jnp.arange(leaf_count)
    slab_index = (leaves // 8).astype(jnp.float32)
    depth_index = (leaves // 4 % 2).astype(jnp.float32)
    row_index = (leaves // 2 % 2).astype(jnp.float32)
    column_index = (leaves % 2).astype(jnp.float32)
    abscissa = (column_index[:, None] + samples[0]) * 0.5
    ordinate = (row_index[:, None] + samples[1]) * 0.5
    altitude = slab_index[:, None] + (depth_index[:, None] + samples[2]) * 0.5
    return jnp.stack([abscissa, ordinate, altitude]).reshape(3, NPTS)


def levels(stream_key, shape, pieces, low, largest):
    level = 1.0
    for dim, blocks in pieces:
        steps = jax.random.uniform(jax.random.fold_in(jax.random.fold_in(stream_key, 6), dim), (blocks,), jnp.float32, low / len(pieces), largest / len(pieces))
        level = level * jnp.repeat(jnp.exp(steps), shape[dim] // blocks).reshape((-1,) + (1,) * (len(shape) - 1 - dim))
    return level


def split_up(amount, total, bound, slope):
    loads = [(1 << 20) // math.isqrt(rank ** slope) + 1 for rank in range(2, amount + 1)]
    surplus, given = total - bound - (amount - 1), [1] * (amount - 1)
    while surplus > 0:
        candidates = [i for i in range(amount - 1) if given[i] < bound]
        mass, left = sum([loads[i] for i in candidates]), surplus
        for i in candidates:
            more = min(bound - given[i], max(1, left * loads[i] // mass), surplus)
            given[i] = given[i] + more
            surplus = surplus - more
    return np.array([bound] + given)


def ragged_sizes(stream_key, amount, total, bound, lean):
    if amount == 2:
        one = jax.random.randint(stream_key, (), max(1, total - bound), min(bound, total - 1) + 1)
        return jnp.stack([one, total - one])
    tallies = jnp.asarray(split_up(amount, total, bound, lean), jnp.int32)
    couples = (amount - 1) // 2
    source_of, receiver = tallies[1:1 + 2 * couples:2], tallies[2:2 + 2 * couples:2]
    room = jnp.minimum(source_of - 1, bound - receiver)
    passed = jax.random.randint(jax.random.fold_in(stream_key, 1), (couples,), 0, 1 << 20) % (room + 1)
    tallies = tallies.at[1:1 + 2 * couples:2].set(source_of - passed).at[2:2 + 2 * couples:2].set(receiver + passed)
    return tallies[jax.random.permutation(jax.random.fold_in(stream_key, 2), amount)]


def gaussian(rng, dims, width, bound, pieces=(), kind=jnp.bfloat16):
    gain = levels(rng, dims, pieces, -0.22, 0.18) if pieces else 1.0
    entries = jax.random.normal(rng, dims, jnp.float32) * width * gain
    return jnp.minimum(jnp.maximum(entries, -bound), bound).astype(kind)


def setup_inputs(seed: int = 0) -> dict:
    key_list = jax.random.split(jax.random.key(seed), 4)
    points = draw_points(jax.random.fold_in(key_list[3], 71), 0)
    vectors = gaussian(key_list[1], (VECS, NPTS), 1.0, 6.0, ((1, 256),), jnp.float32)
    counts = jax.vmap(lambda own: ragged_sizes(own, 8, 6 * LEAF_PTS, LEAF_PTS, 2))(jax.random.split(key_list[2], NSLAB)).reshape((NSLAB, 8)).astype(jnp.int32)
    return dict(points=points, vectors=vectors, counts=counts)


TERM_SCALE = 1.0 / 32.0
ROOT_THREE = math.sqrt(3.0)
far_offsets = (-3, -2, 2, 3)
far_sources = ((0, (0, 4, 5)), (1, (0, 1, 5)))
slab_group = 16

def term_lengths(slab_count):
    term_count = (slab_count.bit_length() - 1) // 3 + 1
    return [slab_count / 4.0 / 8.0 ** term_index for term_index in range(term_count)]

def chebyshev(order):
    return np.cos((2.0 * np.arange(order) + 1.0) * np.pi / (2.0 * order))

def lagrange_table(values, node_values):
    columns = []
    for anchor in range(len(node_values)):
        product = values * 0.0 + 1.0
        for against in range(len(node_values)):
            if against != anchor:
                product = product * (values - node_values[against]) / (node_values[anchor] - node_values[against])
        columns.append(product)
    return np.stack(columns, -1)

def lagrange_values(values, node_values):
    columns = []
    for anchor in range(len(node_values)):
        product = jnp.ones_like(values)
        for against in range(len(node_values)):
            if against != anchor:
                factor = 1.0 / float(node_values[anchor] - node_values[against])
                product = product * ((values - float(node_values[against])) * factor)
        columns.append(product)
    return jnp.stack(columns, -1)

def grid_nodes(node_values):
    number = len(node_values)
    along_z, along_y, along_x = np.meshgrid(np.arange(number), np.arange(number), np.arange(number), indexing='ij')
    return np.stack([node_values[along_x.ravel()], node_values[along_y.ravel()], node_values[along_z.ravel()]], -1)

def kernel_table(targets, sources, lengths):
    offsets_xyz = targets[:, None, :] - sources[None, :, :]
    distance = np.sqrt(np.sum(offsets_xyz * offsets_xyz, -1))
    summed_terms = distance * 0.0
    for length in lengths:
        scaled = distance * (ROOT_THREE / length)
        summed_terms = summed_terms + TERM_SCALE / math.sqrt(length) * (1.0 + scaled) * np.exp(-scaled)
    return summed_terms

def kernel_values(squared, lengths):
    distance = jnp.sqrt(squared)
    summed_terms = jnp.zeros_like(distance)
    for length in lengths:
        scaled = distance * (ROOT_THREE / length)
        summed_terms = summed_terms + TERM_SCALE / math.sqrt(length) * (1.0 + scaled) * jnp.exp(-scaled)
    return summed_terms

def child_tables(node_values):
    halves = [lagrange_table(side_offset + 0.5 * node_values, node_values) for side_offset in (-0.5, 0.5)]
    identity = np.eye(len(node_values))
    octant_rows = []
    for depth_index in range(2):
        for row_index in range(2):
            for column_index in range(2):
                octant_rows.append(np.kron(np.kron(halves[depth_index], halves[row_index]), halves[column_index]))
    octant_array = np.stack(octant_rows).reshape((2, 2, 2) + octant_rows[0].shape)
    half_array = np.stack([np.kron(np.kron(halves[half_index], identity), identity) for half_index in range(2)])
    return (octant_array, half_array)

def leaf_coupling(node_values, depth_index, layer_index, lengths):
    scaled = grid_nodes(node_values) * 0.25
    targets = []
    sources = []
    for row_index in range(2):
        for column_index in range(2):
            targets.append(scaled + np.array([(column_index + 0.5) * 0.5, (row_index + 0.5) * 0.5, (depth_index + 0.5) * 0.5]))
            sources.append(scaled + np.array([(column_index + 0.5) * 0.5, (row_index + 0.5) * 0.5, (layer_index - 1.5) * 0.5]))
    return kernel_table(np.concatenate(targets), np.concatenate(sources), lengths)

def coarse_couplings(node_values, height, lengths):
    span = float(1 << height)
    targets = grid_nodes(node_values) * np.array([0.5, 0.5, 0.5 * span])
    return np.stack([kernel_table(targets, targets + np.array([0.0, 0.0, offset * span]), lengths) for offset in far_offsets])

def basis_of(coords, first_slab, node_values):
    layer_ids = jnp.arange(coords.shape[1])
    slab_of = (first_slab + layer_ids // 2).astype(coords.dtype)
    depth_centre = ((layer_ids % 2).astype(coords.dtype) + 0.5) * 0.5
    centre = (jnp.arange(2).astype(coords.dtype) + 0.5) * 0.5
    along_width = (coords[0] - centre[None, None, :, None]) * 4.0
    along_height = (coords[1] - centre[None, :, None, None]) * 4.0
    along_depth = (coords[2] - slab_of[:, None, None, None] - depth_centre[:, None, None, None]) * 4.0
    poly_width = lagrange_values(along_width, node_values)
    poly_height = lagrange_values(along_height, node_values)
    poly_depth = lagrange_values(along_depth, node_values)
    combined = poly_depth[..., :, None, None] * poly_height[..., None, :, None] * poly_width[..., None, None, :]
    return combined.reshape(combined.shape[:4] + (-1,))

def near_field(window, targets, lengths):
    layer_count = targets.shape[1]
    padded = jnp.pad(window, ((0, 0), (0, 0), (1, 1), (1, 1), (0, 0)))
    summed = jnp.zeros((window.shape[0] - 3,) + targets.shape[1:], window.dtype)
    for step_depth in (-1, 0, 1):
        for step_height in (-1, 0, 1):
            for step_width in (-1, 0, 1):
                source = padded[:, 1 + step_depth:1 + step_depth + layer_count, 1 + step_height:3 + step_height, 1 + step_width:3 + step_width]
                squared = (targets[0][..., :, None] - source[0][..., None, :]) ** 2 + (targets[1][..., :, None] - source[1][..., None, :]) ** 2 + (targets[2][..., :, None] - source[2][..., None, :]) ** 2
                weights = kernel_values(squared, lengths)
                summed = summed + jnp.einsum('zyxij,vzyxj->vzyxi', weights, source[3:], precision=lax.Precision.HIGHEST)
    return summed

def leaf_far(window, node_values, lengths):
    pair_count = (window.shape[0] - 4) // 2
    rank_count = window.shape[3]
    vector_count = window.shape[4]
    stacked = []
    for depth_index, layer_list in far_sources:
        summed = jnp.zeros((pair_count, 4 * rank_count, vector_count), window.dtype)
        for layer_index in layer_list:
            coupling = jnp.asarray(leaf_coupling(node_values, depth_index, layer_index, lengths), jnp.float32)
            source = window[layer_index:layer_index + 2 * pair_count:2].reshape(pair_count, 4 * rank_count, vector_count)
            summed = summed + jnp.einsum('mn,jnv->jmv', coupling, source, precision=lax.Precision.HIGHEST)
        stacked.append(summed.reshape(pair_count, 2, 2, rank_count, vector_count))
    return jnp.stack(stacked, 1).reshape(2 * pair_count, 2, 2, rank_count, vector_count)

def reference(points, vectors, counts):
    lengths = term_lengths(NSLAB)
    node_values = chebyshev(ORDER)
    octant_array, half_array = child_tables(node_values)
    octants = jnp.asarray(octant_array, jnp.float32)
    half_tables = jnp.asarray(half_array, jnp.float32)
    layers = 2 * NSLAB
    coords = points.reshape(3, layers, 2, 2, LEAF_PTS)
    occupied = (jnp.arange(LEAF_PTS)[None, :] < counts.reshape(-1, 1)).astype(jnp.float32).reshape(layers, 2, 2, LEAF_PTS)
    masked = vectors.reshape(VECS, layers, 2, 2, LEAF_PTS) * occupied
    record = jnp.concatenate([coords, masked], 0)
    leaf_bases = basis_of(coords, 0, node_values)
    leaf_coeffs = jnp.einsum('zyxpr,vzyxp->zyxrv', leaf_bases, masked, precision=lax.Precision.HIGHEST)
    box_table = jnp.einsum('abcmn,sabcmv->snv', octants, leaf_coeffs.reshape(NSLAB, 2, 2, 2, RANK, VECS), precision=lax.Precision.HIGHEST)
    far_terms = []
    for height in range(LEVELS):
        box_count = box_table.shape[0]
        padded = jnp.pad(box_table, ((3, 3), (0, 0), (0, 0)))
        parity = (jnp.arange(box_count) % 2 == 0)[:, None, None]
        couplings = jnp.asarray(coarse_couplings(node_values, height, lengths), jnp.float32)
        summed = jnp.zeros_like(box_table)
        for position, offset in enumerate(far_offsets):
            source = padded[3 + offset:3 + offset + box_count]
            contribution = jnp.einsum('mn,inv->imv', couplings[position], source, precision=lax.Precision.HIGHEST)
            if offset == 3:
                contribution = jnp.where(parity, contribution, 0.0)
            if offset == -3:
                contribution = jnp.where(parity, 0.0, contribution)
            summed = summed + contribution
        far_terms.append(summed)
        if height + 1 < LEVELS:
            paired = box_table.reshape(box_count // 2, 2, RANK, VECS)
            box_table = jnp.einsum('cmn,icmv->inv', half_tables, paired, precision=lax.Precision.HIGHEST)
    local_exp = far_terms[LEVELS - 1]
    for height in range(LEVELS - 2, -1, -1):
        children = jnp.einsum('cmn,inv->icmv', half_tables, local_exp, precision=lax.Precision.HIGHEST)
        local_exp = far_terms[height] + children.reshape(-1, RANK, VECS)
    inherited = jnp.einsum('abcmn,snv->sabcmv', octants, local_exp, precision=lax.Precision.HIGHEST).reshape(layers, 2, 2, RANK, VECS)
    coeff_padded = jnp.pad(leaf_coeffs, ((2, 2), (0, 0), (0, 0), (0, 0), (0, 0)))
    record_padded = jnp.pad(record, ((0, 0), (1, 1), (0, 0), (0, 0), (0, 0)))

    def per_group(group_index):
        first_layer = (2 * slab_group * group_index).astype(jnp.int32)
        coeff_window = lax.dynamic_slice_in_dim(coeff_padded, first_layer, 2 * slab_group + 4, 0)
        near_window = lax.dynamic_slice_in_dim(record_padded, first_layer, 2 * slab_group + 2, 1)
        targets = lax.dynamic_slice_in_dim(coords, first_layer, 2 * slab_group, 1)
        return (leaf_far(coeff_window, node_values, lengths), near_field(near_window, targets, lengths))
    far_leaves, near_terms = lax.map(per_group, jnp.arange(NSLAB // slab_group).astype(jnp.int32))
    leaf_local = inherited + far_leaves.reshape(layers, 2, 2, RANK, VECS)
    near_term = jnp.transpose(near_terms, (1, 0, 2, 3, 4, 5)).reshape(VECS, layers, 2, 2, LEAF_PTS)
    result = jnp.einsum('zyxpr,zyxrv->vzyxp', leaf_bases, leaf_local, precision=lax.Precision.HIGHEST) + near_term
    return (result * occupied).reshape(VECS, -1)
```

```python
import functools
import math

import jax
import jax.numpy as jnp
import ml_dtypes
import numpy as np
from jax import lax
from jax.experimental import pallas as pl
from jax.experimental.pallas import tpu as pltpu
from jax.sharding import PartitionSpec as P

ORDER = 4
VECS = 32
CUBES = 8
LAYERS = 16
SLOTS = 4096
TOP = 10
ROOT_THREE = math.sqrt(3.0)
AXES = ("leaf", "sub")
F32 = jnp.float32
BF16 = jnp.bfloat16
NN = (((1,), (0,)), ((), ()))
NT = (((1,), (1,)), ((), ()))
NODES = np.cos((2.0 * np.arange(ORDER) + 1.0) * np.pi / (2.0 * ORDER))
LENGTHS = [512.0, 64.0, 8.0, 1.0]
STRETCH = ROOT_THREE / math.log(2.0)
VMEM_LIMIT = 48 * 1024 * 1024


def lagrange_table(values):
    columns = []
    for anchor in range(ORDER):
        product = values * 0.0 + 1.0
        for against in range(ORDER):
            if against != anchor:
                product = product * (values - NODES[against]) / (NODES[anchor] - NODES[against])
        columns.append(product)
    return np.stack(columns, -1)


def grid_nodes():
    z, y, x = np.meshgrid(np.arange(ORDER), np.arange(ORDER), np.arange(ORDER), indexing="ij")
    return np.stack([NODES[x.ravel()], NODES[y.ravel()], NODES[z.ravel()]], -1)


def kernel_table(targets, sources):
    gaps = targets[:, None, :] - sources[None, :, :]
    distance = np.sqrt(np.sum(gaps * gaps, -1))
    total = distance * 0.0
    for length in LENGTHS:
        scaled = distance * (ROOT_THREE / length)
        total = total + (1.0 + scaled) * np.exp(-scaled) / (32.0 * math.sqrt(length))
    return total


def layer_nodes(layer):
    scaled = grid_nodes() * 0.25
    leaves = []
    for row in range(2):
        for column in range(2):
            centre = [(column + 0.5) * 0.5, (row + 0.5) * 0.5, (layer + 0.5) * 0.5]
            leaves.append(scaled + np.array(centre))
    return np.concatenate(leaves)


def pair_coupling(level):
    span = float(1 << level)
    nodes = grid_nodes() * np.array([0.5, 0.5, 0.5 * span])

    def block(offset):
        return kernel_table(nodes, nodes + np.array([0.0, 0.0, offset * span])).T

    zero = np.zeros((64, 64))
    before = np.block([[block(-2), block(-3)], [zero, block(-2)]])
    after = np.block([[block(2), zero], [block(3), block(2)]])
    return np.concatenate([before, after], 0)


def transfer_tables():
    halves = [lagrange_table(side + 0.5 * NODES) for side in (-0.5, 0.5)]
    eye = np.eye(ORDER)
    octants = [
        np.kron(np.kron(halves[z], halves[y]), halves[x])
        for z in range(2)
        for y in range(2)
        for x in range(2)
    ]
    along = [np.kron(np.kron(half, eye), eye) for half in halves]
    return np.concatenate(octants, 0), np.concatenate(along, 0)


def hi_lo(table):
    high = table.astype(ml_dtypes.bfloat16)
    low = (table - high.astype(np.float64)).astype(ml_dtypes.bfloat16)
    return jnp.asarray(high), jnp.asarray(low)


def split(x):
    high = x.astype(BF16)
    return high, (x - high.astype(F32)).astype(BF16)


def mxu(a, b, dims=NN):
    return lax.dot_general(a, b, dims, preferred_element_type=F32)


def dot3(x, high, low, dims=NN):
    rows = x.shape[0]
    x_high, x_low = split(x)
    both = mxu(jnp.concatenate([x_high, x_low], 0), high, dims)
    return both[:rows] + both[rows:] + mxu(x_high, low, dims)


def poly4(u):
    gaps = [u - float(node) for node in NODES]
    polys = []
    for anchor in range(ORDER):
        scale = 1.0
        product = None
        for against in range(ORDER):
            if against != anchor:
                scale = scale / float(NODES[anchor] - NODES[against])
                product = gaps[against] if product is None else product * gaps[against]
        polys.append(product * scale)
    return polys


def basis64(u):
    count = u.shape[1]
    polys = poly4(u)
    row = lax.broadcasted_iota(jnp.int32, (16, count), 0)

    def picked(dim, key):
        rows = [jnp.broadcast_to(poly[dim : dim + 1], (16, count)) for poly in polys]
        low = jnp.where(key == 0, rows[0], rows[1])
        high = jnp.where(key == 2, rows[2], rows[3])
        return jnp.where(key < 2, low, high)

    plane = picked(0, row % 4) * picked(1, row // 4)
    return jnp.concatenate([plane * poly[2:3] for poly in polys], 0)


def stack_rows(x, width):
    return jnp.concatenate(
        [x[:, i * width : (i + 1) * width] for i in range(x.shape[1] // width)], 0
    )


def pair_rows(boxes):
    count = boxes.shape[0] // VECS
    parts = [boxes[i * VECS : (i + 1) * VECS] for i in range(count)]
    return jnp.concatenate(
        [jnp.concatenate(parts[i : i + 2], 1) for i in range(0, count, 2)], 0
    )


def unpair_rows(pairs):
    count = pairs.shape[0] // VECS
    parts = []
    for i in range(count):
        block = pairs[i * VECS : (i + 1) * VECS]
        parts += [block[:, :64], block[:, 64:]]
    return jnp.concatenate(parts, 0)


def pack_box(box):
    return jnp.concatenate([box[:16], box[16:]], 1)


def unpack_box(packed):
    return jnp.concatenate([packed[:, :64], packed[:, 64:]], 0)


def features(coords, origin):
    row = lax.broadcasted_iota(jnp.int32, coords.shape, 0)
    q = (coords - jnp.where(row == 2, origin, 0.0)) * STRETCH
    norm = jnp.sum(q * q, axis=0, keepdims=True)
    left = jnp.where(row == 3, norm, jnp.where(row == 4, 1.0, q))
    right = jnp.where(row == 3, 1.0, jnp.where(row == 4, norm, -2.0 * q))
    return left, right


def three_parts(x):
    first = x.astype(BF16).astype(F32)
    rest = x - first
    second = rest.astype(BF16).astype(F32)
    return first, second, rest - second


def left_side(left):
    f1, f2, f3 = three_parts(left)
    return jnp.concatenate([f1, f1, f2, f2, f1, f3], 0)


def right_side(right):
    g1, g2, g3 = three_parts(right)
    return jnp.concatenate([g1, g2, g1, g2, g3, g1], 0).astype(BF16)


def matern(squared):
    squared = jnp.maximum(squared, 1e-20)
    w = squared * lax.rsqrt(squared)
    total = None
    for length in LENGTHS:
        weight = 1.0 / (32.0 * math.sqrt(length))
        slope = weight * math.log(2.0) / length
        term = (weight + slope * w) * jnp.exp2(w * (-1.0 / length))
        total = term if total is None else total + term
    return total


def fill_weights(left, right, high_ref, low_ref):
    turned = jnp.transpose(left_side(left)).astype(BF16)
    sources = right_side(right)
    rows, columns = left.shape[1], right.shape[1]
    step = 32
    for top in range(0, rows, step):
        for start in range(0, columns, 256):
            squared = mxu(turned[top : top + step], sources[:, start : start + 256])
            high, low = split(matern(squared))
            high_ref[top : top + step, start : start + 256] = high
            low_ref[top : top + step, start : start + 256] = low


def weigh(x, high, low, dims):
    return dot3(x, high, low, dims)


def head_kernel(slab_ref, counts_ref, points_ref, vectors_ref, coords_ref, masked_ref, occ_ref,
                box_ref, high_ref, low_ref):
    first = slab_ref[0].astype(F32)
    lane = lax.broadcasted_iota(jnp.int32, (1, 512), 1)
    row = lax.broadcasted_iota(jnp.int32, (8, 512), 0)

    def cube(s, total):
        at = pl.ds(pl.multiple_of(s * 512, 512), 512)
        filled = jnp.zeros((1, 512), jnp.int32)
        for c in range(8):
            filled = jnp.where(lane // 64 == c, counts_ref[s, c], filled)
        occupied = (lane % 64 < filled).astype(F32)
        occ_ref[:, at] = occupied
        masked = vectors_ref[:, at] * occupied
        masked_ref[:, at] = masked
        points = points_ref[:, at]
        points = jnp.concatenate([points, jnp.zeros((5, 512), F32)], 0)
        shift = jnp.where(row == 2, first, jnp.where(row < 2, 0.5, 0.0))
        coords = points - shift
        coords_ref[:, at] = coords
        u = (coords - jnp.where(row == 2, 4.0, 0.0)) * jnp.where(row == 2, 0.25, 2.0)
        high, low = split(basis64(u))
        high_ref[:, at] = high
        low_ref[:, at] = low
        return total + dot3(masked, high, low, NT)

    total = lax.fori_loop(0, CUBES, cube, jnp.zeros((VECS, 64), F32))
    box_ref[...] = pack_box(total)


def spread_basis(high, low):
    lane = lax.broadcasted_iota(jnp.int32, (1, 256), 1)
    highs, lows = [], []
    for leaf in range(4):
        mask = (lane // 64 == leaf).astype(F32).astype(BF16)
        highs.append(high * mask)
        lows.append(low * mask)
    return jnp.concatenate(highs, 0), jnp.concatenate(lows, 0)


def leaf_kernel(coords_ref, masked_ref, octh_ref, octl_ref, lifth_ref, liftl_ref, coef_ref,
                high_ref, low_ref, p0_ref, p1_ref, p2_ref, ahead_ref, behind_ref):
    lane = lax.broadcasted_iota(jnp.int32, (8, 256), 1)
    row = lax.broadcasted_iota(jnp.int32, (8, 256), 0)
    centre_x = jnp.where(lane // 64 % 2 == 0, -0.25, 0.25)
    centre_y = jnp.where(lane // 128 == 0, -0.25, 0.25)

    def layer(z, carry):
        at = pl.ds(pl.multiple_of(z * 256, 256), 256)
        centre_z = z.astype(F32) * 0.5 + 0.25
        centre = jnp.where(row == 0, centre_x, jnp.where(row == 1, centre_y, centre_z))
        u = (coords_ref[:, at] - centre) * 4.0
        high, low = split(basis64(u))
        high_ref[:, at] = high
        low_ref[:, at] = low
        wide_high, wide_low = spread_basis(high, low)
        coef_ref[:, at] = dot3(masked_ref[:, at], wide_high, wide_low, NT)
        return carry

    lax.fori_loop(0, LAYERS, layer, 0)
    boxes = dot3(stack_rows(coef_ref[...], 512), octh_ref[...], octl_ref[...])
    p0 = pair_rows(boxes)
    p1 = pair_rows(dot3(p0, lifth_ref[...], liftl_ref[...]))
    p2 = pair_rows(dot3(p1, lifth_ref[...], liftl_ref[...]))
    p0_ref[...] = p0
    p1_ref[...] = p1
    p2_ref[...] = p2
    for ref, near, far, low_pair, mid_pair in (
        (ahead_ref, SLOTS - 256, SLOTS - 512, p0[96:], p1[32:]),
        (behind_ref, 0, 0, p0[:32], p1[:32]),
    ):
        ref[:, 0:256] = masked_ref[:, near : near + 256]
        ref[:, 256:768] = coef_ref[:, far : far + 512]
        ref[:, 768:896] = low_pair
        ref[:, 896:1024] = mid_pair
        ref[:, 1024:1152] = p2
        ref[:, 1152:1280] = jnp.zeros((VECS, 128), F32)
        ref[0:8, 1152:1280] = coords_ref[:, near : near + 128]
        ref[8:16, 1152:1280] = coords_ref[:, near + 128 : near + 256]


def near_kernel(begin, end, coords_ref, masked_ref, before_ref, hold_ref, near_ref, high_ref,
                low_ref):
    del hold_ref
    near_ref[...] = before_ref[...] if begin else jnp.zeros_like(near_ref)

    def layer(z, carry):
        own = pl.ds(pl.multiple_of(z * 256, 256), 256)
        both = pl.ds(pl.multiple_of(z * 256, 256), 512)
        after = pl.ds(pl.multiple_of(z * 256 + 256, 256), 256)
        left, right = features(coords_ref[:, both], z.astype(F32) * 0.5 + 0.5)
        fill_weights(left[:, :256], right, high_ref, low_ref)
        x = masked_ref[:, own]
        summed = weigh(x, high_ref[...], low_ref[...], NN)
        back = weigh(masked_ref[:, after], high_ref[:, 256:], low_ref[:, 256:], NT)
        near_ref[:, own] += summed[:, :256] + back
        near_ref[:, after] += summed[:, 256:]
        return carry

    lax.fori_loop(begin, min(end, LAYERS - 1), layer, 0)
    if end == LAYERS:
        left, right = features(coords_ref[:, SLOTS - 256 :], LAYERS / 2.0)
        fill_weights(left, right, high_ref, low_ref)
        near_ref[:, SLOTS - 256 :] += weigh(
            masked_ref[:, SLOTS - 256 :], high_ref[:, :256], low_ref[:, :256], NN
        )


def gather_kernel(member_ref, a_ref, b_ref, c_ref, d_ref, lifth_ref, liftl_ref, hold_ref,
                  quad_ref, pair_ref, box_ref, ahead_ref, behind_ref, slots):
    del hold_ref
    member = member_ref[0]
    for step, ref in enumerate((a_ref, b_ref, c_ref, d_ref)):
        slots[pl.ds(member ^ step, 1)] = unpack_box(ref[...])[None]
    left = jnp.concatenate([slots[0], slots[1]], 1)
    right = jnp.concatenate([slots[2], slots[3]], 1)
    quad_ref[...] = jnp.concatenate([left, right], 1)
    lifted = dot3(jnp.concatenate([left, right], 0), lifth_ref[...], liftl_ref[...])
    pair = pair_rows(lifted)
    pair_ref[...] = pair
    box_ref[...] = pack_box(dot3(pair, lifth_ref[...], liftl_ref[...]))
    ahead_ref[...] = jnp.concatenate([right, pair], 1)
    behind_ref[...] = jnp.concatenate([left, pair], 1)


def rim_kernel(coords_ref, masked_ref, near_ref, coef_ref, basish_ref, basisl_ref, p0_ref, p1_ref,
               p2_ref, left_ref, right_ref, k2h_ref, k2l_ref, k3h_ref, k3l_ref, m0h_ref, m0l_ref,
               m1h_ref, m1l_ref, m2h_ref, m2l_ref, sinkh_ref, sinkl_ref, octh_ref, octl_ref,
               hold_ref, base_ref, high_ref, low_ref):
    del hold_ref
    base_ref[...] = near_ref[...]
    row = lax.broadcasted_iota(jnp.int32, (8, 256), 0)

    def rim_coords(ref, shift):
        coords = jnp.concatenate([ref[0:8, 1152:1280], ref[8:16, 1152:1280]], 1)
        return coords + jnp.where(row == 2, shift, 0.0)

    low_rim = rim_coords(left_ref, -float(CUBES))
    left, _ = features(low_rim, 0.0)
    _, right = features(coords_ref[:, :256], 0.0)
    fill_weights(left, right, high_ref, low_ref)
    base_ref[:, :256] += weigh(left_ref[:, :256], high_ref[...], low_ref[...], NN)
    high_rim = rim_coords(right_ref, float(CUBES))
    left, _ = features(coords_ref[:, SLOTS - 256 :], float(CUBES))
    _, right = features(high_rim, float(CUBES))
    fill_weights(left, right, high_ref, low_ref)
    base_ref[:, SLOTS - 256 :] += weigh(right_ref[:, :256], high_ref[...], low_ref[...], NT)

    coefs = [coef_ref[:, 512 * s : 512 * s + 512] for s in range(CUBES)]
    before = jnp.concatenate([left_ref[:, 256:768]] + coefs[:-1], 0)
    after = jnp.concatenate(coefs[1:] + [right_ref[:, 256:768]], 0)
    k2 = (k2h_ref[...], k2l_ref[...])
    k3 = (k3h_ref[...], k3l_ref[...])
    even = dot3(before[:, :256], *k2) + dot3(after[:, :256], *k2, NT) + dot3(after[:, 256:], *k3, NT)
    odd = dot3(before[:, :256], *k3) + dot3(before[:, 256:], *k2) + dot3(after[:, 256:], *k2, NT)

    def coupled(pairs, lower, upper, high, low):
        sides = jnp.concatenate(
            [
                jnp.concatenate([lower, pairs[:-VECS]], 0) if pairs.shape[0] > VECS else lower,
                jnp.concatenate([pairs[VECS:], upper], 0) if pairs.shape[0] > VECS else upper,
            ],
            1,
        )
        return dot3(sides, high, low)

    sink = (sinkh_ref[...], sinkl_ref[...])
    local = coupled(p2_ref[...], left_ref[:, 1024:1152], right_ref[:, 1024:1152], m2h_ref[...], m2l_ref[...])
    local = coupled(
        p1_ref[...], left_ref[:, 896:1024], right_ref[:, 896:1024], m1h_ref[...], m1l_ref[...]
    ) + dot3(unpair_rows(local), *sink)
    local = coupled(
        p0_ref[...], left_ref[:, 768:896], right_ref[:, 768:896], m0h_ref[...], m0l_ref[...]
    ) + dot3(unpair_rows(local), *sink)
    inherited = dot3(unpair_rows(local), octh_ref[...], octl_ref[...], NT)
    even = even + inherited[:, :256]
    odd = odd + inherited[:, 256:]
    for s in range(CUBES):
        for part, values in ((0, even), (1, odd)):
            at = slice(512 * s + 256 * part, 512 * s + 256 * part + 256)
            high, low = spread_basis(basish_ref[:, at], basisl_ref[:, at])
            base_ref[:, at] += dot3(values[VECS * s : VECS * s + VECS], high, low)


def tail_kernel(index_ref, base_ref, occ_ref, high_ref, low_ref, boxes_ref, quad3_ref, quad5_ref,
                left3_ref, right3_ref, left5_ref, right5_ref, mh_ref, ml_ref, sinkh_ref, sinkl_ref,
                out_ref):
    index = index_ref[0]
    top = index // 16

    def box7(number):
        inside = ((number >= 0) & (number < 16)).astype(F32)
        safe = jnp.clip(number, 0, 15)
        return unpack_box(boxes_ref[pl.ds(safe ^ top, 1)][0]) * inside

    sink = (sinkh_ref[...], sinkl_ref[...])

    def lift(pairs):
        return pair_rows(dot3(pairs, *sink, NT))

    def level7(pair):
        return jnp.concatenate([box7(2 * pair), box7(2 * pair + 1)], 1)

    sides = {}
    for level, quad_ref, left_ref, right_ref in (
        (3, quad3_ref, left3_ref, right3_ref),
        (5, quad5_ref, left5_ref, right5_ref),
    ):
        is_low = index // (1 << (level - 2)) % 2 == 0
        left, right = left_ref[...], right_ref[...]
        sides[level] = jnp.concatenate(
            [
                jnp.where(is_low, left[:, :128], quad_ref[:, :128]),
                jnp.where(is_low, quad_ref[:, 128:], right[:, :128]),
            ],
            1,
        )
        sides[level + 1] = jnp.concatenate([left[:, 128:], right[:, 128:]], 1)
    pair7 = top // 2
    sides[7] = jnp.concatenate([level7(pair7 - 1), level7(pair7 + 1)], 1)
    pair8 = top // 4
    pairs = [level7(2 * (pair8 + side) + half) for side in (-1, 1) for half in (0, 1)]
    pair9 = 1 - top // 8
    pairs += [level7(4 * pair9 + quarter) for quarter in range(4)]
    lifted = lift(jnp.concatenate(pairs, 0))
    sides[8] = jnp.concatenate([lifted[:VECS], lifted[VECS : 2 * VECS]], 1)
    other = lift(lifted[2 * VECS :])
    is_upper = (pair9 == 0).astype(F32)
    sides[9] = jnp.concatenate([other * is_upper, other * (1.0 - is_upper)], 1)
    local = None
    for level in range(TOP - 1, 2, -1):
        far = dot3(sides[level], mh_ref[level - 3], ml_ref[level - 3])
        if local is not None:
            far = far + dot3(local, *sink)
        is_low = index // (1 << (level - 3)) % 2 == 0
        local = jnp.where(is_low, far[:, :64], far[:, 64:])
    out_ref[...] = (base_ref[...] + dot3(local, high_ref[...], low_ref[...])) * occ_ref[...]


VMEM = pl.BlockSpec(memory_space=pltpu.VMEM)
SMEM = pl.BlockSpec(memory_space=pltpu.SMEM)
ANY = pl.BlockSpec(memory_space=pl.ANY)


def call(body, in_specs, outs, scratch=(), aliases=None, name=None):
    return pl.pallas_call(
        body,
        out_shape=[jax.ShapeDtypeStruct(shape, dtype) for shape, dtype in outs],
        in_specs=in_specs,
        out_specs=[VMEM] * len(outs),
        scratch_shapes=list(scratch),
        input_output_aliases=aliases or {},
        compiler_params=pltpu.CompilerParams(vmem_limit_bytes=VMEM_LIMIT),
        name=name,
    )


def local(points, vectors, counts):
    devices = lax.axis_size(AXES)
    index = lax.axis_index(AXES).astype(jnp.int32)

    def crossed(value, mask):
        return lax.ppermute(value, AXES, [(i, i ^ mask) for i in range(devices)])

    def shifted(value, by):
        pairs = [(i, i + by) for i in range(devices) if 0 <= i + by < devices]
        return lax.ppermute(value, AXES, pairs)

    octants, along = transfer_tables()
    octants = hi_lo(octants)
    lift = hi_lo(along)
    sink = hi_lo(along.T)
    k2 = hi_lo(kernel_table(layer_nodes(0), layer_nodes(2)))
    k3 = hi_lo(kernel_table(layer_nodes(0), layer_nodes(3)))
    low_tables = [table for level in range(3) for table in hi_lo(pair_coupling(level))]
    high_tables = hi_lo(np.stack([pair_coupling(level) for level in range(3, TOP)]))

    coords, masked, occupied, box3, far_high, far_low = call(
        head_kernel,
        [SMEM, SMEM, VMEM, VMEM],
        [
            ((8, SLOTS), F32),
            ((VECS, SLOTS), F32),
            ((1, SLOTS), F32),
            ((16, 128), F32),
            ((64, SLOTS), BF16),
            ((64, SLOTS), BF16),
        ],
        name="head",
    )((index * CUBES)[None], counts, points, vectors)

    def gathered(box, bit, hold):
        others = [crossed(box, step << bit) for step in (1, 2, 3)]
        return call(
            gather_kernel,
            [SMEM] + [VMEM] * 6 + [ANY],
            [
                ((VECS, 256), F32),
                ((VECS, 128), F32),
                ((16, 128), F32),
                ((VECS, 256), F32),
                ((VECS, 256), F32),
            ],
            [pltpu.VMEM((4, VECS, 64), F32)],
            name="gather",
        )((index >> bit & 3)[None], box, *others, *lift, hold)

    def near_part(before, begin, end, hold):
        return call(
            functools.partial(near_kernel, begin, end),
            [VMEM] * 3 + [ANY],
            [((VECS, SLOTS), F32)],
            [pltpu.VMEM((256, 512), BF16), pltpu.VMEM((256, 512), BF16)],
            aliases={2: 0},
            name="near",
        )(coords, masked, before, hold)[0]

    coef, leaf_high, leaf_low, p0, p1, p2, ahead, behind = call(
        leaf_kernel,
        [VMEM] * 6,
        [
            ((VECS, SLOTS), F32),
            ((64, SLOTS), BF16),
            ((64, SLOTS), BF16),
            ((4 * VECS, 128), F32),
            ((2 * VECS, 128), F32),
            ((VECS, 128), F32),
            ((VECS, 1280), F32),
            ((VECS, 1280), F32),
        ],
        name="leaf",
    )(coords, masked, *octants, *lift)
    from_left = shifted(ahead, 1)
    from_right = shifted(behind, -1)
    quad3, _, box5, ahead3, behind3 = gathered(box3, 0, p2)
    left3 = shifted(ahead3, 4)
    right3 = shifted(behind3, -4)
    near = near_part(masked, 0, 5, quad3)
    quad5, _, box7, ahead5, behind5 = gathered(box5, 2, near)
    left5 = shifted(ahead5, 16)
    right5 = shifted(behind5, -16)
    near = near_part(near, 5, 9, quad5)
    boxes = jnp.stack([box7, crossed(box7, 16)])
    near = near_part(near, 9, 13, boxes)
    boxes = jnp.concatenate([boxes, crossed(boxes, 32)], 0)
    near = near_part(near, 13, 16, boxes)
    boxes = jnp.concatenate([boxes, crossed(boxes, 64)], 0)
    base = call(
        rim_kernel,
        [VMEM] * 25 + [ANY],
        [((VECS, SLOTS), F32)],
        [pltpu.VMEM((256, 256), BF16), pltpu.VMEM((256, 256), BF16)],
        aliases={2: 0},
        name="rim",
    )(
        coords, masked, near, coef, leaf_high, leaf_low, p0, p1, p2, from_left, from_right,
        *k2, *k3, *low_tables, *sink, *octants, boxes,
    )[0]
    boxes = jnp.concatenate([boxes, crossed(boxes, 128)], 0)
    return call(
        tail_kernel,
        [SMEM] + [VMEM] * 15,
        [((VECS, SLOTS), F32)],
        aliases={1: 0},
        name="tail",
    )(
        index[None], base, occupied, far_high, far_low, boxes, quad3, quad5, left3, right3, left5,
        right5, *high_tables, *sink,
    )[0]


def solution(mesh):
    in_specs = (P(None, AXES), P(None, AXES), P(AXES, None))
    return jax.shard_map(
        local, mesh=mesh, in_specs=in_specs, out_specs=P(None, AXES), check_vma=False
    )
```

```python
import functools
import math

import jax
import jax.numpy as jnp
import ml_dtypes
import numpy as np
from jax import lax
from jax.experimental import pallas as pl
from jax.experimental.pallas import tpu as pltpu
from jax.sharding import PartitionSpec as P

ORDER = 4
VECS = 32
CUBES = 8
LAYERS = 16
SLOTS = 4096
TOP = 10
ROOT_THREE = math.sqrt(3.0)
AXES = ("leaf", "sub")
F32 = jnp.float32
BF16 = jnp.bfloat16
NN = (((1,), (0,)), ((), ()))
NT = (((1,), (1,)), ((), ()))
NODES = np.cos((2.0 * np.arange(ORDER) + 1.0) * np.pi / (2.0 * ORDER))
LENGTHS = [512.0, 64.0, 8.0, 1.0]
STRETCH = ROOT_THREE / math.log(2.0)
VMEM_LIMIT = 16 * 1024 * 1024


def lagrange_table(values):
    columns = []
    for anchor in range(ORDER):
        product = values * 0.0 + 1.0
        for against in range(ORDER):
            if against != anchor:
                product = product * (values - NODES[against]) / (NODES[anchor] - NODES[against])
        columns.append(product)
    return np.stack(columns, -1)


def grid_nodes():
    z, y, x = np.meshgrid(np.arange(ORDER), np.arange(ORDER), np.arange(ORDER), indexing="ij")
    return np.stack([NODES[x.ravel()], NODES[y.ravel()], NODES[z.ravel()]], -1)


def kernel_table(targets, sources):
    gaps = targets[:, None, :] - sources[None, :, :]
    distance = np.sqrt(np.sum(gaps * gaps, -1))
    total = distance * 0.0
    for length in LENGTHS:
        scaled = distance * (ROOT_THREE / length)
        total = total + (1.0 + scaled) * np.exp(-scaled) / (32.0 * math.sqrt(length))
    return total


def layer_nodes(layer):
    scaled = grid_nodes() * 0.25
    leaves = []
    for row in range(2):
        for column in range(2):
            centre = [(column + 0.5) * 0.5, (row + 0.5) * 0.5, (layer + 0.5) * 0.5]
            leaves.append(scaled + np.array(centre))
    return np.concatenate(leaves)


def pair_coupling(level):
    span = float(1 << level)
    nodes = grid_nodes() * np.array([0.5, 0.5, 0.5 * span])

    def block(offset):
        return kernel_table(nodes, nodes + np.array([0.0, 0.0, offset * span])).T

    zero = np.zeros((64, 64))
    before = np.block([[block(-2), block(-3)], [zero, block(-2)]])
    after = np.block([[block(2), zero], [block(3), block(2)]])
    return np.concatenate([before, after], 0)


def transfer_tables():
    halves = [lagrange_table(side + 0.5 * NODES) for side in (-0.5, 0.5)]
    eye = np.eye(ORDER)
    octants = [
        np.kron(np.kron(halves[z], halves[y]), halves[x])
        for z in range(2)
        for y in range(2)
        for x in range(2)
    ]
    along = [np.kron(np.kron(half, eye), eye) for half in halves]
    return np.concatenate(octants, 0), np.concatenate(along, 0)


def hi_lo(table):
    high = table.astype(ml_dtypes.bfloat16)
    low = (table - high.astype(np.float64)).astype(ml_dtypes.bfloat16)
    return np.stack([high, low])


def split(x):
    high = x.astype(BF16)
    return high, (x - high.astype(F32)).astype(BF16)


def mxu(a, b, dims=NN):
    return lax.dot_general(a, b, dims, preferred_element_type=F32)


def dot3(x, high, low, dims=NN):
    rows = x.shape[0]
    x_high, x_low = split(x)
    both = mxu(jnp.concatenate([x_high, x_low], 0), high, dims)
    return both[:rows] + both[rows:] + mxu(x_high, low, dims)


def poly4(u):
    gaps = [u - float(node) for node in NODES]
    polys = []
    for anchor in range(ORDER):
        scale = 1.0
        product = None
        for against in range(ORDER):
            if against != anchor:
                scale = scale / float(NODES[anchor] - NODES[against])
                product = gaps[against] if product is None else product * gaps[against]
        polys.append(product * scale)
    return polys


def basis64(u):
    count = u.shape[1]
    polys = poly4(u)
    row = lax.broadcasted_iota(jnp.int32, (16, count), 0)

    def picked(dim, key):
        rows = [jnp.broadcast_to(poly[dim : dim + 1], (16, count)) for poly in polys]
        low = jnp.where(key == 0, rows[0], rows[1])
        high = jnp.where(key == 2, rows[2], rows[3])
        return jnp.where(key < 2, low, high)

    plane = picked(0, row % 4) * picked(1, row // 4)
    return jnp.concatenate([plane * poly[2:3] for poly in polys], 0)


def stack_rows(x, width):
    return jnp.concatenate(
        [x[:, i * width : (i + 1) * width] for i in range(x.shape[1] // width)], 0
    )


def pair_rows(boxes):
    count = boxes.shape[0] // VECS
    parts = [boxes[i * VECS : (i + 1) * VECS] for i in range(count)]
    return jnp.concatenate(
        [jnp.concatenate(parts[i : i + 2], 1) for i in range(0, count, 2)], 0
    )


def unpair_rows(pairs):
    count = pairs.shape[0] // VECS
    parts = []
    for i in range(count):
        block = pairs[i * VECS : (i + 1) * VECS]
        parts += [block[:, :64], block[:, 64:]]
    return jnp.concatenate(parts, 0)


def pack_box(box):
    return jnp.concatenate([box[:16], box[16:]], 1)


def unpack_box(packed):
    return jnp.concatenate([packed[:, :64], packed[:, 64:]], 0)


def features(coords, origin):
    row = lax.broadcasted_iota(jnp.int32, coords.shape, 0)
    q = (coords - jnp.where(row == 2, origin, 0.0)) * STRETCH
    norm = jnp.sum(q * q, axis=0, keepdims=True)
    left = jnp.where(row == 3, norm, jnp.where(row == 4, 1.0, q))
    right = jnp.where(row == 3, 1.0, jnp.where(row == 4, norm, -2.0 * q))
    return left, right


def three_parts(x):
    first = x.astype(BF16).astype(F32)
    rest = x - first
    second = rest.astype(BF16).astype(F32)
    return first, second, rest - second


def left_side(left):
    f1, f2, f3 = three_parts(left)
    return jnp.concatenate([f1, f1, f2, f2, f1, f3], 0)


def right_side(right):
    g1, g2, g3 = three_parts(right)
    return jnp.concatenate([g1, g2, g1, g2, g3, g1], 0).astype(BF16)


def matern(squared):
    squared = jnp.maximum(squared, 1e-20)
    w = squared * lax.rsqrt(squared)
    total = None
    for length in LENGTHS:
        weight = 1.0 / (32.0 * math.sqrt(length))
        slope = weight * math.log(2.0) / length
        term = (weight + slope * w) * jnp.exp2(w * (-1.0 / length))
        total = term if total is None else total + term
    return total


def fill_weights(turned, sources, high_ref, low_ref, top=0, begin=0):
    rows, columns = turned.shape[0], sources.shape[1]
    step = 128
    for row in range(0, rows, step):
        values = matern(mxu(turned[row : row + step], sources))
        high, low = split(values)
        at = slice(top + row, top + row + step), slice(begin, begin + columns)
        high_ref[at] = high
        low_ref[at] = low


def turned_side(left):
    return jnp.transpose(left_side(left)).astype(BF16)


def head_kernel(slab_ref, counts_hbm, points_hbm, vectors_hbm, coords_ref, masked_ref, occ_ref,
                box_ref, high_ref, low_ref, counts_ref, points_ref, vectors_ref, sems):
    first = slab_ref[0].astype(F32)
    lane = lax.broadcasted_iota(jnp.int32, (1, 512), 1)
    row = lax.broadcasted_iota(jnp.int32, (8, 512), 0)
    copies = [
        pltpu.make_async_copy(counts_hbm, counts_ref, sems.at[0]),
        pltpu.make_async_copy(points_hbm, points_ref, sems.at[1]),
    ]
    half = SLOTS // 2
    for part in range(2):
        at = slice(part * half, part * half + half)
        copies.append(
            pltpu.make_async_copy(vectors_hbm.at[:, at], vectors_ref.at[:, at], sems.at[2 + part])
        )
    for copy in copies:
        copy.start()

    def cube(s, total):
        at = pl.ds(pl.multiple_of(s * 512, 512), 512)
        filled = jnp.zeros((1, 512), jnp.int32)
        for c in range(8):
            filled = jnp.where(lane // 64 == c, counts_ref[s, c], filled)
        occupied = (lane % 64 < filled).astype(F32)
        occ_ref[:, at] = occupied
        masked = vectors_ref[:, at] * occupied
        masked_ref[:, at] = masked
        points = points_ref[:, at]
        points = jnp.concatenate([points, jnp.zeros((5, 512), F32)], 0)
        shift = jnp.where(row == 2, first, jnp.where(row < 2, 0.5, 0.0))
        coords = points - shift
        coords_ref[:, at] = coords
        u = (coords - jnp.where(row == 2, 4.0, 0.0)) * jnp.where(row == 2, 0.25, 2.0)
        high, low = split(basis64(u))
        high_ref[:, at] = high
        low_ref[:, at] = low
        return total + dot3(masked, high, low, NT)

    for copy in copies[:3]:
        copy.wait()
    total = lax.fori_loop(0, CUBES // 2, cube, jnp.zeros((VECS, 64), F32))
    copies[3].wait()
    total = lax.fori_loop(CUBES // 2, CUBES, cube, total)
    box_ref[...] = pack_box(total)


def spread_basis(high, low):
    lane = lax.broadcasted_iota(jnp.int32, (1, 256), 1)
    highs, lows = [], []
    for leaf in range(4):
        mask = (lane // 64 == leaf).astype(F32).astype(BF16)
        highs.append(high * mask)
        lows.append(low * mask)
    return jnp.concatenate(highs, 0), jnp.concatenate(lows, 0)


def leaf_kernel(index_ref, coords_ref, masked_ref, octants_ref, sink_ref, coef_ref, high_ref,
                low_ref, pairs_ref, facing_ref, away_ref):
    lane = lax.broadcasted_iota(jnp.int32, (8, 256), 1)
    row = lax.broadcasted_iota(jnp.int32, (8, 256), 0)
    centre_x = jnp.where(lane // 64 % 2 == 0, -0.25, 0.25)
    centre_y = jnp.where(lane // 128 == 0, -0.25, 0.25)

    def layer(z, carry):
        at = pl.ds(pl.multiple_of(z * 256, 256), 256)
        centre_z = z.astype(F32) * 0.5 + 0.25
        centre = jnp.where(row == 0, centre_x, jnp.where(row == 1, centre_y, centre_z))
        u = (coords_ref[:, at] - centre) * 4.0
        high, low = split(basis64(u))
        high_ref[:, at] = high
        low_ref[:, at] = low
        wide_high, wide_low = spread_basis(high, low)
        coef_ref[:, at] = dot3(masked_ref[:, at], wide_high, wide_low, NT)
        return carry

    lax.fori_loop(0, LAYERS, layer, 0)
    boxes = dot3(stack_rows(coef_ref[...], 512), octants_ref[0], octants_ref[1], NT)
    p0 = pair_rows(boxes)
    p1 = pair_rows(dot3(p0, sink_ref[0], sink_ref[1], NT))
    p2 = pair_rows(dot3(p1, sink_ref[0], sink_ref[1], NT))
    pairs_ref[...] = jnp.concatenate([p0, p1, p2], 0)

    def bundle(ref, near, far, low_pair, mid_pair):
        ref[:, 0:256] = masked_ref[:, near : near + 256]
        ref[:, 256:768] = coef_ref[:, far : far + 512]
        ref[:, 768:896] = low_pair
        ref[:, 896:1024] = mid_pair
        ref[:, 1024:1152] = p2
        ref[:, 1152:1280] = jnp.zeros((VECS, 128), F32)
        ref[0:8, 1152:1280] = coords_ref[:, near : near + 128]
        ref[8:16, 1152:1280] = coords_ref[:, near + 128 : near + 256]

    is_even = index_ref[0] % 2 == 0

    @pl.when(is_even)
    def _():
        bundle(facing_ref, SLOTS - 256, SLOTS - 512, p0[96:], p1[32:])
        bundle(away_ref, 0, 0, p0[:32], p1[:32])

    @pl.when(jnp.logical_not(is_even))
    def _():
        bundle(away_ref, SLOTS - 256, SLOTS - 512, p0[96:], p1[32:])
        bundle(facing_ref, 0, 0, p0[:32], p1[:32])


def near_kernel(begin, end, coords_ref, masked_ref, hold_ref, near_ref, own_high, own_low,
                next_high, next_low, turned_ref):
    del hold_ref
    near_ref[...] = jnp.zeros_like(near_ref)

    def out(z):
        return pl.ds(pl.multiple_of((z - begin) * 256, 256), 256)

    def lanes(z):
        return pl.ds(pl.multiple_of(z * 256, 256), 256)

    def top_of(z):
        return jnp.asarray(z, F32) * 0.5 + 0.5

    def fill_own(z):
        left, right = features(coords_ref[:, lanes(z)], top_of(z))
        turned = turned_side(left)
        turned_ref[...] = turned
        sources = right_side(right)
        fill_weights(turned[:128], sources, own_high, own_low)
        fill_weights(turned[128:], sources[:, 128:], own_high, own_low, 128, 128)

    def fill_next(z):
        _, right = features(coords_ref[:, lanes(z + 1)], top_of(z))
        fill_weights(turned_ref[...], right_side(right), next_high, next_low)

    def add_own(z):
        x = masked_ref[:, lanes(z)]
        both = dot3(x[:, :128], own_high[:128], own_low[:128])
        first = dot3(x[:, 128:], own_high[:128, 128:], own_low[:128, 128:], NT)
        second = dot3(x[:, 128:], own_high[128:, 128:], own_low[128:, 128:])
        near_ref[:, out(z)] += both + jnp.concatenate([first, second], 1)

    def add_next(z):
        near_ref[:, out(z)] += dot3(masked_ref[:, lanes(z + 1)], next_high[...], next_low[...], NT)
        near_ref[:, out(z + 1)] += dot3(masked_ref[:, lanes(z)], next_high[...], next_low[...])

    def layer(z, carry):
        fill_next(z)
        add_own(z)
        fill_own(z + 1)
        add_next(z)
        return carry

    fill_own(begin)
    lax.fori_loop(begin, end - 1, layer, 0)
    if end < LAYERS:
        fill_next(end - 1)
    add_own(end - 1)
    if end < LAYERS:
        add_next(end - 1)


def four_to_one(slots, sink_ref):
    left = jnp.concatenate([slots[0], slots[1]], 1)
    right = jnp.concatenate([slots[2], slots[3]], 1)
    lifted = dot3(jnp.concatenate([left, right], 0), sink_ref[0], sink_ref[1], NT)
    pair = pair_rows(lifted)
    box = pack_box(dot3(pair, sink_ref[0], sink_ref[1], NT))
    return left, right, pair, box


def lower_gather_kernel(index_ref, own_ref, far_ref, sink_ref, hold_ref, quad_ref, close_ref,
                        wide_ref, slots):
    del hold_ref
    index = index_ref[0]
    for step, box in enumerate((own_ref[0], own_ref[1], far_ref[0], far_ref[1])):
        slots[pl.ds(index % 4 ^ step, 1)] = unpack_box(box)[None]
    left, right, pair, box = four_to_one(slots, sink_ref)
    quad_ref[...] = jnp.concatenate([left, right], 1)
    is_even = index // 4 % 2 == 0
    facing = jnp.where(is_even, right, left)
    away = jnp.where(is_even, left, right)
    close_ref[...] = jnp.concatenate([box, facing, pair, away, pair], 0)
    wide_ref[...] = jnp.concatenate([box, away, pair], 0)


def upper_gather_kernel(index_ref, own_ref, one_ref, two_ref, three_ref, sink_ref, hold_ref,
                        quad_ref, box_ref, inside_ref, close_ref, wide_ref, slots, edges):
    del hold_ref
    index = index_ref[0]
    member = index // 4 % 4
    for step, ref in enumerate((own_ref, one_ref, two_ref, three_ref)):
        slots[pl.ds(member ^ step, 1)] = unpack_box(ref[:16])[None]
        edges[pl.ds(member ^ step, 1)] = ref[80:144][None] if step == 1 else ref[16:80][None]
    left, right, pair, box = four_to_one(slots, sink_ref)
    quad_ref[...] = jnp.concatenate([left, right], 1)
    box_ref[...] = box
    beside, across = one_ref[16:80], three_ref[16:80]
    is_odd = member % 2 == 1
    inside_ref[:64] = jnp.where(is_odd, beside, across)
    inside_ref[64:] = jnp.where(is_odd, across, beside)
    is_even = index // 16 % 2 == 0
    first, last = edges[0], edges[3]
    facing = jnp.where(is_even, right, left)
    away = jnp.where(is_even, left, right)
    close_ref[...] = jnp.concatenate([box, facing, pair, jnp.where(is_even, last, first)], 0)
    wide_ref[...] = jnp.concatenate([away, pair, jnp.where(is_even, first, last)], 0)


def rim_kernel(parts, index_ref, coords_ref, masked_ref, coef_ref, basish_ref, basisl_ref,
               pairs_ref, facing_ref, away_ref, layers_ref, coupling_ref, sink_ref, octants_ref,
               quad3_ref, quad5_ref, inside_ref, close_ref, wide_ref, *refs):
    near_refs = refs[: len(parts)]
    _, base_ref, local_ref, path_ref, high_ref, low_ref, left_ref, right_ref = refs[len(parts) :]
    index = index_ref[0]
    base_ref[...] = jnp.zeros_like(base_ref)
    for (begin, end), ref in zip(parts, near_refs):
        base_ref[:, 256 * begin : 256 * end + 256] += ref[...]
    is_even = index % 2 == 0
    left_ref[...] = jnp.where(is_even, away_ref[...], facing_ref[...])
    right_ref[...] = jnp.where(is_even, facing_ref[...], away_ref[...])
    row = lax.broadcasted_iota(jnp.int32, (8, 256), 0)

    def rim_coords(ref, shift):
        coords = jnp.concatenate([ref[0:8, 1152:1280], ref[8:16, 1152:1280]], 1)
        return coords + jnp.where(row == 2, shift, 0.0)

    low_rim = rim_coords(left_ref, -float(CUBES))
    left, _ = features(low_rim, 0.0)
    _, right = features(coords_ref[:, :256], 0.0)
    fill_weights(turned_side(left), right_side(right), high_ref, low_ref)
    base_ref[:, :256] += dot3(left_ref[:, :256], high_ref[...], low_ref[...], NN)
    high_rim = rim_coords(right_ref, float(CUBES))
    left, _ = features(coords_ref[:, SLOTS - 256 :], float(CUBES))
    _, right = features(high_rim, float(CUBES))
    fill_weights(turned_side(left), right_side(right), high_ref, low_ref)
    base_ref[:, SLOTS - 256 :] += dot3(right_ref[:, :256], high_ref[...], low_ref[...], NT)

    coefs = [coef_ref[:, 512 * s : 512 * s + 512] for s in range(CUBES)]
    before = jnp.concatenate([left_ref[:, 256:768]] + coefs[:-1], 0)
    after = jnp.concatenate(coefs[1:] + [right_ref[:, 256:768]], 0)
    k2 = (layers_ref[0], layers_ref[1])
    k3 = (layers_ref[2], layers_ref[3])
    even = dot3(before[:, :256], *k2) + dot3(after[:, :256], *k2, NT) + dot3(after[:, 256:], *k3, NT)
    odd = dot3(before[:, :256], *k3) + dot3(before[:, 256:], *k2) + dot3(after[:, 256:], *k2, NT)

    def coupled(pairs, level):
        at = slice(768 + 128 * level, 896 + 128 * level)
        lower, upper = left_ref[:, at], right_ref[:, at]
        sides = jnp.concatenate(
            [
                jnp.concatenate([lower, pairs[:-VECS]], 0) if pairs.shape[0] > VECS else lower,
                jnp.concatenate([pairs[VECS:], upper], 0) if pairs.shape[0] > VECS else upper,
            ],
            1,
        )
        return dot3(sides, coupling_ref[2 * level], coupling_ref[2 * level + 1])

    sink = (sink_ref[0], sink_ref[1])
    local = coupled(pairs_ref[6 * VECS :], 2)
    local = coupled(pairs_ref[4 * VECS : 6 * VECS], 1) + dot3(unpair_rows(local), *sink)
    local = coupled(pairs_ref[: 4 * VECS], 0) + dot3(unpair_rows(local), *sink)
    inherited = dot3(unpair_rows(local), octants_ref[0], octants_ref[1])
    even = even + inherited[:, :256]
    odd = odd + inherited[:, 256:]
    for s in range(CUBES):
        for part, values in ((0, even), (1, odd)):
            at = slice(512 * s + 256 * part, 512 * s + 256 * part + 256)
            high, low = spread_basis(basish_ref[:, at], basisl_ref[:, at])
            base_ref[:, at] += dot3(values[VECS * s : VECS * s + VECS], high, low)

    member = index // 4 % 4
    is_even = index // 16 % 2 == 0
    beside, outer = close_ref[...], wide_ref[...]
    left = jnp.where(member == 0, jnp.where(is_even, outer[64:], beside[80:]), inside_ref[:64])
    right = jnp.where(member == 3, jnp.where(is_even, beside[80:], outer[64:]), inside_ref[64:])
    edges = {
        3: (left, right),
        5: (
            jnp.where(is_even, outer[:64], beside[16:80]),
            jnp.where(is_even, beside[16:80], outer[:64]),
        ),
    }

    def is_low(level):
        return index // (1 << (level - 3)) % 2 == 0

    def half(both, level):
        return jnp.where(is_low(level), both[:, :64], both[:, 64:])

    sides = {}
    for level, quad_ref in ((3, quad3_ref), (5, quad5_ref)):
        left, right = edges[level]
        low = is_low(level + 1)
        sides[level] = jnp.concatenate(
            [
                jnp.where(low, left[:VECS], quad_ref[:, :128]),
                jnp.where(low, quad_ref[:, 128:], right[:VECS]),
            ],
            1,
        )
        sides[level + 1] = jnp.concatenate([left[VECS:], right[VECS:]], 1)
    local = path = None
    for level in (6, 5, 4, 3):
        far = dot3(sides[level], coupling_ref[2 * level], coupling_ref[2 * level + 1])
        step = sink[0].astype(F32) + sink[1].astype(F32)
        if local is not None:
            far = far + dot3(local, *sink)
            step = dot3(path, *sink)
        local = half(far, level)
        path = half(step, level)
    local_ref[...] = local
    path_ref[...] = path


def tail_kernel(begin, index_ref, base_ref, near_ref, occ_ref, high_ref, low_ref, boxes_ref,
                far_ref, local_ref, path_ref, coupling_ref, sink_ref, out_ref):
    index = index_ref[0]
    top = index // 16
    count = boxes_ref.shape[0]

    def box7(number):
        inside = ((number >= 0) & (number < 16)).astype(F32)
        place = jnp.clip(number, 0, 15) ^ top
        at = pl.ds(place % count, 1)
        packed = jnp.where(place < count, boxes_ref[at][0], far_ref[at][0])
        return unpack_box(packed) * inside

    sink = (sink_ref[0], sink_ref[1])

    def lift(pairs):
        return pair_rows(dot3(pairs, *sink, NT))

    def level7(pair):
        return jnp.concatenate([box7(2 * pair), box7(2 * pair + 1)], 1)

    sides = {}
    pair7 = top // 2
    sides[7] = jnp.concatenate([level7(pair7 - 1), level7(pair7 + 1)], 1)
    pair8 = top // 4
    pairs = [level7(2 * (pair8 + side) + half) for side in (-1, 1) for half in (0, 1)]
    pair9 = 1 - top // 8
    pairs += [level7(4 * pair9 + quarter) for quarter in range(4)]
    lifted = lift(jnp.concatenate(pairs, 0))
    sides[8] = jnp.concatenate([lifted[:VECS], lifted[VECS : 2 * VECS]], 1)
    other = lift(lifted[2 * VECS :])
    is_upper = (pair9 == 0).astype(F32)
    sides[9] = jnp.concatenate([other * is_upper, other * (1.0 - is_upper)], 1)
    local = None
    for level in (9, 8, 7):
        far = dot3(sides[level], coupling_ref[2 * level - 14], coupling_ref[2 * level - 13])
        if local is not None:
            far = far + dot3(local, *sink)
        is_low = index // (1 << (level - 3)) % 2 == 0
        local = jnp.where(is_low, far[:, :64], far[:, 64:])
    local = local_ref[...] + dot3(local, *split(path_ref[...]))
    split_at = 256 * begin
    far = dot3(local, high_ref[...], low_ref[...])
    out_ref[...] = (base_ref[...] + far) * occ_ref[...]
    out_ref[:, split_at:] += near_ref[...] * occ_ref[:, split_at:]


VMEM = pl.BlockSpec(memory_space=pltpu.VMEM)
SMEM = pl.BlockSpec(memory_space=pltpu.SMEM)
HBM = pl.BlockSpec(memory_space=pltpu.HBM)
ANY = pl.BlockSpec(memory_space=pl.ANY)


def call(body, in_specs, outs, scratch=(), aliases=None, name=None):
    return pl.pallas_call(
        body,
        out_shape=[jax.ShapeDtypeStruct(shape, dtype) for shape, dtype in outs],
        in_specs=in_specs,
        out_specs=[VMEM] * len(outs),
        scratch_shapes=list(scratch),
        input_output_aliases=aliases or {},
        compiler_params=pltpu.CompilerParams(vmem_limit_bytes=VMEM_LIMIT),
        name=name,
    )


def local(points, vectors, counts):
    devices = lax.axis_size(AXES)
    index = lax.axis_index(AXES).astype(jnp.int32)

    def crossed(value, mask):
        return lax.ppermute(value, AXES, [(i, i ^ mask) for i in range(devices)])

    def swapped(value, size):
        pairs = []
        for i in range(size, devices - size):
            pairs.append((i, i + size if i // size % 2 else i - size))
        return lax.ppermute(value, AXES, pairs)

    def after(value, *others):
        return lax.optimization_barrier((value,) + others)[0]

    octants, along = transfer_tables()
    octants = jnp.asarray(hi_lo(octants.T))
    sink = jnp.asarray(hi_lo(along.T))
    layers = jnp.asarray(
        np.concatenate([hi_lo(kernel_table(layer_nodes(0), layer_nodes(z))) for z in (2, 3)])
    )
    couplings = [hi_lo(pair_coupling(level)) for level in range(TOP)]
    low_couplings = jnp.asarray(np.concatenate(couplings[:7]))
    high_couplings = jnp.asarray(np.concatenate(couplings[7:]))

    coords, masked, occupied, box3, far_high, far_low = call(
        head_kernel,
        [SMEM, HBM, HBM, HBM],
        [
            ((8, SLOTS), F32),
            ((VECS, SLOTS), F32),
            ((1, SLOTS), F32),
            ((16, 128), F32),
            ((64, SLOTS), BF16),
            ((64, SLOTS), BF16),
        ],
        [
            pltpu.SMEM((CUBES, 8), jnp.int32),
            pltpu.VMEM((3, SLOTS), F32),
            pltpu.VMEM((VECS, SLOTS), F32),
            pltpu.SemaphoreType.DMA((4,)),
        ],
        name="head",
    )((index * CUBES)[None], counts, points, vectors)

    number = index[None]

    def near_part(part, hold):
        own = pltpu.VMEM((256, 256), BF16)
        begin, end = part
        width = 256 * (min(end + 1, LAYERS) - begin)
        return call(
            functools.partial(near_kernel, begin, end),
            [VMEM, VMEM, ANY],
            [((VECS, width), F32)],
            [own] * 4 + [pltpu.VMEM((256, 48), BF16)],
            name="near",
        )(coords, masked, hold)[0]

    parts = [(0, 4), (4, 6), (6, 10), (10, 13)]
    last = (13, 16)
    arrived = crossed(box3, 1)
    coef, leaf_high, leaf_low, pairs, facing, away = call(
        leaf_kernel,
        [SMEM] + [VMEM] * 4,
        [
            ((VECS, SLOTS), F32),
            ((64, SLOTS), BF16),
            ((64, SLOTS), BF16),
            ((7 * VECS, 128), F32),
            ((VECS, 1280), F32),
            ((VECS, 1280), F32),
        ],
        name="leaf",
    )(number, coords, masked, octants, sink)
    boxes3 = jnp.stack([box3, after(arrived, pairs)])
    arrived = crossed(boxes3, 2)
    near = [near_part(parts[0], boxes3)]
    slots = pltpu.VMEM((4, VECS, 64), F32)
    quad3, close3, wide3 = call(
        lower_gather_kernel,
        [SMEM] + [VMEM] * 3 + [ANY],
        [((VECS, 256), F32), ((144, 128), F32), ((80, 128), F32)],
        [slots],
        name="gather3",
    )(number, boxes3, arrived, sink, near[-1])
    others = [crossed(close3, 4), crossed(wide3, 8), crossed(wide3, 12)]
    near.append(near_part(parts[1], wide3))
    quad5, box7, inside, close5, wide5 = call(
        upper_gather_kernel,
        [SMEM] + [VMEM] * 5 + [ANY],
        [
            ((VECS, 256), F32),
            ((16, 128), F32),
            ((128, 128), F32),
            ((144, 128), F32),
            ((128, 128), F32),
        ],
        [slots, pltpu.VMEM((4, 64, 128), F32)],
        name="gather5",
    )(number, wide3, *others, sink, near[-1])
    beside5 = crossed(close5, 16)
    facing = crossed(after(facing, box7), 1)
    near.append(near_part(parts[2], box7))
    boxes = jnp.stack([box7, after(beside5, near[-1])[:16]])
    arrived = crossed(boxes, 32)
    away = swapped(after(away, boxes), 1)
    outer5 = swapped(after(wide5, boxes), 16)
    near.append(near_part(parts[3], boxes))
    boxes = jnp.concatenate([boxes, after(arrived, near[-1])], 0)
    arrived = crossed(boxes, 64)
    halo = pltpu.VMEM((VECS, 1280), F32)
    base, far_local, path = call(
        functools.partial(rim_kernel, parts),
        [SMEM] + [VMEM] * (17 + len(parts)) + [ANY],
        [((VECS, SLOTS), F32), ((VECS, 64), F32), ((64, 64), F32)],
        [pltpu.VMEM((256, 256), BF16)] * 2 + [halo] * 2,
        name="rim",
    )(
        number, coords, masked, coef, leaf_high, leaf_low, pairs, facing, away, layers,
        low_couplings, sink, octants, quad3, quad5, inside, beside5, outer5, *near, boxes,
    )
    boxes = jnp.concatenate([boxes, after(arrived, base)], 0)
    arrived = crossed(boxes, 128)
    final = near_part(last, boxes)
    return call(
        functools.partial(tail_kernel, last[0]),
        [SMEM] + [VMEM] * 11,
        [((VECS, SLOTS), F32)],
        name="tail",
    )(
        number, base, final, occupied, far_high, far_low, boxes, after(arrived, final), far_local,
        path, high_couplings, sink,
    )[0]


def solution(mesh):
    in_specs = (P(None, AXES), P(None, AXES), P(AXES, None))
    return jax.shard_map(
        local, mesh=mesh, in_specs=in_specs, out_specs=P(None, AXES), check_vma=False
    )
```

```python
import functools
import math

import jax
import jax.numpy as jnp
import ml_dtypes
import numpy as np
from jax import lax
from jax.experimental import pallas as pl
from jax.experimental.pallas import tpu as pltpu
from jax.sharding import PartitionSpec as P

ORDER = 4
VECS = 32
CUBES = 8
LAYERS = 16
SLOTS = 4096
TOP = 10
ROOT_THREE = math.sqrt(3.0)
AXES = ("leaf", "sub")
F32 = jnp.float32
BF16 = jnp.bfloat16
NN = (((1,), (0,)), ((), ()))
NT = (((1,), (1,)), ((), ()))
NODES = np.cos((2.0 * np.arange(ORDER) + 1.0) * np.pi / (2.0 * ORDER))
LENGTHS = [512.0, 64.0, 8.0, 1.0]
STRETCH = ROOT_THREE / math.log(2.0)
VMEM_LIMIT = 16 * 1024 * 1024


def lagrange_table(values):
    columns = []
    for anchor in range(ORDER):
        product = values * 0.0 + 1.0
        for against in range(ORDER):
            if against != anchor:
                product = product * (values - NODES[against]) / (NODES[anchor] - NODES[against])
        columns.append(product)
    return np.stack(columns, -1)


def grid_nodes():
    z, y, x = np.meshgrid(np.arange(ORDER), np.arange(ORDER), np.arange(ORDER), indexing="ij")
    return np.stack([NODES[x.ravel()], NODES[y.ravel()], NODES[z.ravel()]], -1)


def kernel_table(targets, sources):
    gaps = targets[:, None, :] - sources[None, :, :]
    distance = np.sqrt(np.sum(gaps * gaps, -1))
    total = distance * 0.0
    for length in LENGTHS:
        scaled = distance * (ROOT_THREE / length)
        total = total + (1.0 + scaled) * np.exp(-scaled) / (32.0 * math.sqrt(length))
    return total


def layer_nodes(layer):
    scaled = grid_nodes() * 0.25
    leaves = []
    for row in range(2):
        for column in range(2):
            centre = [(column + 0.5) * 0.5, (row + 0.5) * 0.5, (layer + 0.5) * 0.5]
            leaves.append(scaled + np.array(centre))
    return np.concatenate(leaves)


def pair_coupling(level):
    span = float(1 << level)
    nodes = grid_nodes() * np.array([0.5, 0.5, 0.5 * span])

    def block(offset):
        return kernel_table(nodes, nodes + np.array([0.0, 0.0, offset * span])).T

    zero = np.zeros((64, 64))
    before = np.block([[block(-2), block(-3)], [zero, block(-2)]])
    after = np.block([[block(2), zero], [block(3), block(2)]])
    return np.concatenate([before, after], 0)


def transfer_tables():
    halves = [lagrange_table(side + 0.5 * NODES) for side in (-0.5, 0.5)]
    eye = np.eye(ORDER)
    octants = [
        np.kron(np.kron(halves[z], halves[y]), halves[x])
        for z in range(2)
        for y in range(2)
        for x in range(2)
    ]
    along = [np.kron(np.kron(half, eye), eye) for half in halves]
    return np.concatenate(octants, 0), np.concatenate(along, 0)


def hi_lo(table):
    high = table.astype(ml_dtypes.bfloat16)
    low = (table - high.astype(np.float64)).astype(ml_dtypes.bfloat16)
    return np.stack([high, low])


def split(x):
    high = x.astype(BF16)
    return high, (x - high.astype(F32)).astype(BF16)


def mxu(a, b, dims=NN):
    return lax.dot_general(a, b, dims, preferred_element_type=F32)


def dot3(x, high, low, dims=NN):
    rows = x.shape[0]
    x_high, x_low = split(x)
    both = mxu(jnp.concatenate([x_high, x_low], 0), high, dims)
    return both[:rows] + both[rows:] + mxu(x_high, low, dims)


def poly4(u):
    gaps = [u - float(node) for node in NODES]
    polys = []
    for anchor in range(ORDER):
        scale = 1.0
        product = None
        for against in range(ORDER):
            if against != anchor:
                scale = scale / float(NODES[anchor] - NODES[against])
                product = gaps[against] if product is None else product * gaps[against]
        polys.append(product * scale)
    return polys


def basis64(u):
    count = u.shape[1]
    polys = poly4(u)
    row = lax.broadcasted_iota(jnp.int32, (16, count), 0)

    def picked(dim, key):
        rows = [jnp.broadcast_to(poly[dim : dim + 1], (16, count)) for poly in polys]
        low = jnp.where(key == 0, rows[0], rows[1])
        high = jnp.where(key == 2, rows[2], rows[3])
        return jnp.where(key < 2, low, high)

    plane = picked(0, row % 4) * picked(1, row // 4)
    return jnp.concatenate([plane * poly[2:3] for poly in polys], 0)


def stack_rows(x, width):
    return jnp.concatenate(
        [x[:, i * width : (i + 1) * width] for i in range(x.shape[1] // width)], 0
    )


def pair_rows(boxes):
    count = boxes.shape[0] // VECS
    parts = [boxes[i * VECS : (i + 1) * VECS] for i in range(count)]
    return jnp.concatenate(
        [jnp.concatenate(parts[i : i + 2], 1) for i in range(0, count, 2)], 0
    )


def unpair_rows(pairs):
    count = pairs.shape[0] // VECS
    parts = []
    for i in range(count):
        block = pairs[i * VECS : (i + 1) * VECS]
        parts += [block[:, :64], block[:, 64:]]
    return jnp.concatenate(parts, 0)


def pack_box(box):
    return jnp.concatenate([box[:16], box[16:]], 1)


def unpack_box(packed):
    return jnp.concatenate([packed[:, :64], packed[:, 64:]], 0)


def features(coords, origin):
    row = lax.broadcasted_iota(jnp.int32, coords.shape, 0)
    q = (coords - jnp.where(row == 2, origin, 0.0)) * STRETCH
    norm = jnp.sum(q * q, axis=0, keepdims=True)
    left = jnp.where(row == 3, norm, jnp.where(row == 4, 1.0, q))
    right = jnp.where(row == 3, 1.0, jnp.where(row == 4, norm, -2.0 * q))
    return left, right


def three_parts(x):
    first = x.astype(BF16).astype(F32)
    rest = x - first
    second = rest.astype(BF16).astype(F32)
    return first, second, rest - second


def left_side(left):
    f1, f2, f3 = three_parts(left)
    return jnp.concatenate([f1, f1, f2, f2, f1, f3], 0)


def right_side(right):
    g1, g2, g3 = three_parts(right)
    return jnp.concatenate([g1, g2, g1, g2, g3, g1], 0).astype(BF16)


def matern(squared):
    squared = jnp.maximum(squared, 1e-20)
    w = squared * lax.rsqrt(squared)
    total = None
    for length in LENGTHS:
        weight = 1.0 / (32.0 * math.sqrt(length))
        slope = weight * math.log(2.0) / length
        term = (weight + slope * w) * jnp.exp2(w * (-1.0 / length))
        total = term if total is None else total + term
    return total


def fill_weights(turned, sources, high_ref, low_ref, top=0, begin=0):
    rows, columns = turned.shape[0], sources.shape[1]
    step = 128
    for row in range(0, rows, step):
        values = matern(mxu(turned[row : row + step], sources))
        high, low = split(values)
        at = slice(top + row, top + row + step), slice(begin, begin + columns)
        high_ref[at] = high
        low_ref[at] = low


def turned_side(left):
    return jnp.transpose(left_side(left)).astype(BF16)


def head_kernel(slab_ref, counts_hbm, points_hbm, vectors_hbm, coords_ref, masked_ref, occ_ref,
                box_ref, high_ref, low_ref, counts_ref, points_ref, vectors_ref, sems):
    first = slab_ref[0].astype(F32)
    lane = lax.broadcasted_iota(jnp.int32, (1, 512), 1)
    row = lax.broadcasted_iota(jnp.int32, (8, 512), 0)
    copies = [
        pltpu.make_async_copy(counts_hbm, counts_ref, sems.at[0]),
        pltpu.make_async_copy(points_hbm, points_ref, sems.at[1]),
    ]
    half = SLOTS // 2
    for part in range(2):
        at = slice(part * half, part * half + half)
        copies.append(
            pltpu.make_async_copy(vectors_hbm.at[:, at], vectors_ref.at[:, at], sems.at[2 + part])
        )
    for copy in copies:
        copy.start()

    def cube(s, total):
        at = pl.ds(pl.multiple_of(s * 512, 512), 512)
        filled = jnp.zeros((1, 512), jnp.int32)
        for c in range(8):
            filled = jnp.where(lane // 64 == c, counts_ref[s, c], filled)
        occupied = (lane % 64 < filled).astype(F32)
        occ_ref[:, at] = occupied
        masked = vectors_ref[:, at] * occupied
        masked_ref[:, at] = masked
        points = points_ref[:, at]
        points = jnp.concatenate([points, jnp.zeros((5, 512), F32)], 0)
        shift = jnp.where(row == 2, first, jnp.where(row < 2, 0.5, 0.0))
        coords = points - shift
        coords_ref[:, at] = coords
        u = (coords - jnp.where(row == 2, 4.0, 0.0)) * jnp.where(row == 2, 0.25, 2.0)
        high, low = split(basis64(u))
        high_ref[:, at] = high
        low_ref[:, at] = low
        return total + dot3(masked, high, low, NT)

    for copy in copies[:3]:
        copy.wait()
    total = lax.fori_loop(0, CUBES // 2, cube, jnp.zeros((VECS, 64), F32), unroll=2)
    copies[3].wait()
    total = lax.fori_loop(CUBES // 2, CUBES, cube, total, unroll=2)
    box_ref[...] = pack_box(total)


def spread_basis(high, low):
    lane = lax.broadcasted_iota(jnp.int32, (1, 256), 1)
    highs, lows = [], []
    for leaf in range(4):
        mask = (lane // 64 == leaf).astype(F32).astype(BF16)
        highs.append(high * mask)
        lows.append(low * mask)
    return jnp.concatenate(highs, 0), jnp.concatenate(lows, 0)


def leaf_kernel(index_ref, coords_ref, masked_ref, octants_ref, sink_ref, hold_ref, coef_ref,
                high_ref, low_ref, pairs_ref, facing_ref, away_ref):
    del hold_ref
    lane = lax.broadcasted_iota(jnp.int32, (8, 256), 1)
    row = lax.broadcasted_iota(jnp.int32, (8, 256), 0)
    centre_x = jnp.where(lane // 64 % 2 == 0, -0.25, 0.25)
    centre_y = jnp.where(lane // 128 == 0, -0.25, 0.25)

    def layer(z, carry):
        at = pl.ds(pl.multiple_of(z * 256, 256), 256)
        centre_z = z.astype(F32) * 0.5 + 0.25
        centre = jnp.where(row == 0, centre_x, jnp.where(row == 1, centre_y, centre_z))
        u = (coords_ref[:, at] - centre) * 4.0
        high, low = split(basis64(u))
        high_ref[:, at] = high
        low_ref[:, at] = low
        wide_high, wide_low = spread_basis(high, low)
        coef_ref[:, at] = dot3(masked_ref[:, at], wide_high, wide_low, NT)
        return carry

    lax.fori_loop(0, LAYERS, layer, 0, unroll=4)
    boxes = dot3(stack_rows(coef_ref[...], 512), octants_ref[0], octants_ref[1], NT)
    p0 = pair_rows(boxes)
    p1 = pair_rows(dot3(p0, sink_ref[0], sink_ref[1], NT))
    p2 = pair_rows(dot3(p1, sink_ref[0], sink_ref[1], NT))
    pairs_ref[...] = jnp.concatenate([p0, p1, p2], 0)

    def bundle(ref, near, far, low_pair, mid_pair):
        ref[:, 0:256] = masked_ref[:, near : near + 256]
        ref[:, 256:768] = coef_ref[:, far : far + 512]
        ref[:, 768:896] = low_pair
        ref[:, 896:1024] = mid_pair
        ref[:, 1024:1152] = p2
        ref[:, 1152:1280] = jnp.zeros((VECS, 128), F32)
        ref[0:8, 1152:1280] = coords_ref[:, near : near + 128]
        ref[8:16, 1152:1280] = coords_ref[:, near + 128 : near + 256]

    is_even = index_ref[0] % 2 == 0

    @pl.when(is_even)
    def _():
        bundle(facing_ref, SLOTS - 256, SLOTS - 512, p0[96:], p1[32:])
        bundle(away_ref, 0, 0, p0[:32], p1[:32])

    @pl.when(jnp.logical_not(is_even))
    def _():
        bundle(away_ref, SLOTS - 256, SLOTS - 512, p0[96:], p1[32:])
        bundle(facing_ref, 0, 0, p0[:32], p1[:32])


def near_kernel(begin, end, coords_ref, masked_ref, *refs):
    near_ref, own_high, own_low, next_high, next_low, turned_ref = refs[-6:]
    near_ref[...] = jnp.zeros_like(near_ref)

    def out(z):
        return pl.ds(pl.multiple_of((z - begin) * 256, 256), 256)

    def lanes(z):
        return pl.ds(pl.multiple_of(z * 256, 256), 256)

    def top_of(z):
        return jnp.asarray(z, F32) * 0.5 + 0.5

    def fill_own(z):
        left, right = features(coords_ref[:, lanes(z)], top_of(z))
        turned = turned_side(left)
        turned_ref[...] = turned
        sources = right_side(right)
        fill_weights(turned[:128], sources, own_high, own_low)
        fill_weights(turned[128:], sources[:, 128:], own_high, own_low, 128, 128)

    def fill_next(z):
        _, right = features(coords_ref[:, lanes(z + 1)], top_of(z))
        fill_weights(turned_ref[...], right_side(right), next_high, next_low)

    def add_own(z):
        x = masked_ref[:, lanes(z)]
        both = dot3(x[:, :128], own_high[:128], own_low[:128])
        first = dot3(x[:, 128:], own_high[:128, 128:], own_low[:128, 128:], NT)
        second = dot3(x[:, 128:], own_high[128:, 128:], own_low[128:, 128:])
        near_ref[:, out(z)] += both + jnp.concatenate([first, second], 1)

    def add_next(z):
        near_ref[:, out(z)] += dot3(masked_ref[:, lanes(z + 1)], next_high[...], next_low[...], NT)
        near_ref[:, out(z + 1)] += dot3(masked_ref[:, lanes(z)], next_high[...], next_low[...])

    def layer(z, carry):
        fill_next(z)
        add_own(z)
        fill_own(z + 1)
        add_next(z)
        return carry

    fill_own(begin)
    lax.fori_loop(begin, end - 1, layer, 0)
    if end < LAYERS:
        fill_next(end - 1)
    add_own(end - 1)
    if end < LAYERS:
        add_next(end - 1)


def four_to_one(slots, sink_ref):
    left = jnp.concatenate([slots[0], slots[1]], 1)
    right = jnp.concatenate([slots[2], slots[3]], 1)
    lifted = dot3(jnp.concatenate([left, right], 0), sink_ref[0], sink_ref[1], NT)
    pair = pair_rows(lifted)
    box = pack_box(dot3(pair, sink_ref[0], sink_ref[1], NT))
    return left, right, pair, box


def lower_gather_kernel(index_ref, own_ref, far_ref, sink_ref, hold_ref, quad_ref, close_ref,
                        wide_ref, slots):
    del hold_ref
    index = index_ref[0]
    for step, box in enumerate((own_ref[0], own_ref[1], far_ref[0], far_ref[1])):
        slots[pl.ds(index % 4 ^ step, 1)] = unpack_box(box)[None]
    left, right, pair, box = four_to_one(slots, sink_ref)
    quad_ref[...] = jnp.concatenate([left, right], 1)
    is_even = index // 4 % 2 == 0
    facing = jnp.where(is_even, right, left)
    away = jnp.where(is_even, left, right)
    close_ref[...] = jnp.concatenate([box, facing, pair, away, pair], 0)
    wide_ref[...] = jnp.concatenate([box, away, pair], 0)


def upper_gather_kernel(index_ref, own_ref, one_ref, two_ref, three_ref, sink_ref, hold_ref,
                        quad_ref, box_ref, inside_ref, close_ref, wide_ref, slots, edges):
    del hold_ref
    index = index_ref[0]
    member = index // 4 % 4
    for step, ref in enumerate((own_ref, one_ref, two_ref, three_ref)):
        slots[pl.ds(member ^ step, 1)] = unpack_box(ref[:16])[None]
        edges[pl.ds(member ^ step, 1)] = ref[80:144][None] if step == 1 else ref[16:80][None]
    left, right, pair, box = four_to_one(slots, sink_ref)
    quad_ref[...] = jnp.concatenate([left, right], 1)
    box_ref[...] = box
    beside, across = one_ref[16:80], three_ref[16:80]
    is_odd = member % 2 == 1
    inside_ref[:64] = jnp.where(is_odd, beside, across)
    inside_ref[64:] = jnp.where(is_odd, across, beside)
    is_even = index // 16 % 2 == 0
    first, last = edges[0], edges[3]
    facing = jnp.where(is_even, right, left)
    away = jnp.where(is_even, left, right)
    close_ref[...] = jnp.concatenate([box, facing, pair, jnp.where(is_even, last, first)], 0)
    wide_ref[...] = jnp.concatenate([away, pair, jnp.where(is_even, first, last)], 0)


def rim_kernel(parts, index_ref, coords_ref, masked_ref, coef_ref, basish_ref, basisl_ref,
               pairs_ref, facing_ref, away_ref, layers_ref, coupling_ref, sink_ref, octants_ref,
               quad3_ref, quad5_ref, inside_ref, close_ref, wide_ref, *refs):
    near_refs = refs[: len(parts)]
    _, base_ref, local_ref, path_ref, high_ref, low_ref, left_ref, right_ref = refs[len(parts) :]
    index = index_ref[0]
    base_ref[...] = jnp.zeros_like(base_ref)
    for (begin, end), ref in zip(parts, near_refs):
        base_ref[:, 256 * begin : min(256 * end + 256, SLOTS)] += ref[...]
    is_even = index % 2 == 0
    left_ref[...] = jnp.where(is_even, away_ref[...], facing_ref[...])
    right_ref[...] = jnp.where(is_even, facing_ref[...], away_ref[...])
    row = lax.broadcasted_iota(jnp.int32, (8, 256), 0)

    def rim_coords(ref, shift):
        coords = jnp.concatenate([ref[0:8, 1152:1280], ref[8:16, 1152:1280]], 1)
        return coords + jnp.where(row == 2, shift, 0.0)

    low_rim = rim_coords(left_ref, -float(CUBES))
    left, _ = features(low_rim, 0.0)
    _, right = features(coords_ref[:, :256], 0.0)
    fill_weights(turned_side(left), right_side(right), high_ref, low_ref)
    base_ref[:, :256] += dot3(left_ref[:, :256], high_ref[...], low_ref[...], NN)
    high_rim = rim_coords(right_ref, float(CUBES))
    left, _ = features(coords_ref[:, SLOTS - 256 :], float(CUBES))
    _, right = features(high_rim, float(CUBES))
    fill_weights(turned_side(left), right_side(right), high_ref, low_ref)
    base_ref[:, SLOTS - 256 :] += dot3(right_ref[:, :256], high_ref[...], low_ref[...], NT)

    coefs = [coef_ref[:, 512 * s : 512 * s + 512] for s in range(CUBES)]
    before = jnp.concatenate([left_ref[:, 256:768]] + coefs[:-1], 0)
    after = jnp.concatenate(coefs[1:] + [right_ref[:, 256:768]], 0)
    k2 = (layers_ref[0], layers_ref[1])
    k3 = (layers_ref[2], layers_ref[3])
    even = dot3(before[:, :256], *k2) + dot3(after[:, :256], *k2, NT) + dot3(after[:, 256:], *k3, NT)
    odd = dot3(before[:, :256], *k3) + dot3(before[:, 256:], *k2) + dot3(after[:, 256:], *k2, NT)

    def coupled(pairs, level):
        at = slice(768 + 128 * level, 896 + 128 * level)
        lower, upper = left_ref[:, at], right_ref[:, at]
        sides = jnp.concatenate(
            [
                jnp.concatenate([lower, pairs[:-VECS]], 0) if pairs.shape[0] > VECS else lower,
                jnp.concatenate([pairs[VECS:], upper], 0) if pairs.shape[0] > VECS else upper,
            ],
            1,
        )
        return dot3(sides, coupling_ref[2 * level], coupling_ref[2 * level + 1])

    sink = (sink_ref[0], sink_ref[1])
    local = coupled(pairs_ref[6 * VECS :], 2)
    local = coupled(pairs_ref[4 * VECS : 6 * VECS], 1) + dot3(unpair_rows(local), *sink)
    local = coupled(pairs_ref[: 4 * VECS], 0) + dot3(unpair_rows(local), *sink)
    inherited = dot3(unpair_rows(local), octants_ref[0], octants_ref[1])
    even = even + inherited[:, :256]
    odd = odd + inherited[:, 256:]
    for s in range(CUBES):
        for part, values in ((0, even), (1, odd)):
            at = slice(512 * s + 256 * part, 512 * s + 256 * part + 256)
            high, low = spread_basis(basish_ref[:, at], basisl_ref[:, at])
            base_ref[:, at] += dot3(values[VECS * s : VECS * s + VECS], high, low)

    member = index // 4 % 4
    is_even = index // 16 % 2 == 0
    beside, outer = close_ref[...], wide_ref[...]
    left = jnp.where(member == 0, jnp.where(is_even, outer[64:], beside[80:]), inside_ref[:64])
    right = jnp.where(member == 3, jnp.where(is_even, beside[80:], outer[64:]), inside_ref[64:])
    edges = {
        3: (left, right),
        5: (
            jnp.where(is_even, outer[:64], beside[16:80]),
            jnp.where(is_even, beside[16:80], outer[:64]),
        ),
    }

    def is_low(level):
        return index // (1 << (level - 3)) % 2 == 0

    def half(both, level):
        return jnp.where(is_low(level), both[:, :64], both[:, 64:])

    sides = {}
    for level, quad_ref in ((3, quad3_ref), (5, quad5_ref)):
        left, right = edges[level]
        low = is_low(level + 1)
        sides[level] = jnp.concatenate(
            [
                jnp.where(low, left[:VECS], quad_ref[:, :128]),
                jnp.where(low, quad_ref[:, 128:], right[:VECS]),
            ],
            1,
        )
        sides[level + 1] = jnp.concatenate([left[VECS:], right[VECS:]], 1)
    local = path = None
    for level in (6, 5, 4, 3):
        far = dot3(sides[level], coupling_ref[2 * level], coupling_ref[2 * level + 1])
        step = sink[0].astype(F32) + sink[1].astype(F32)
        if local is not None:
            far = far + dot3(local, *sink)
            step = dot3(path, *sink)
        local = half(far, level)
        path = half(step, level)
    local_ref[...] = local
    path_ref[...] = path


def tail_kernel(index_ref, base_ref, occ_ref, high_ref, low_ref, boxes_ref,
                far_ref, local_ref, path_ref, coupling_ref, sink_ref, out_ref):
    index = index_ref[0]
    top = index // 16
    count = boxes_ref.shape[0]

    def box7(number):
        inside = ((number >= 0) & (number < 16)).astype(F32)
        place = jnp.clip(number, 0, 15) ^ top
        at = pl.ds(place % count, 1)
        packed = jnp.where(place < count, boxes_ref[at][0], far_ref[at][0])
        return unpack_box(packed) * inside

    sink = (sink_ref[0], sink_ref[1])

    def lift(pairs):
        return pair_rows(dot3(pairs, *sink, NT))

    def level7(pair):
        return jnp.concatenate([box7(2 * pair), box7(2 * pair + 1)], 1)

    sides = {}
    pair7 = top // 2
    sides[7] = jnp.concatenate([level7(pair7 - 1), level7(pair7 + 1)], 1)
    pair8 = top // 4
    pairs = [level7(2 * (pair8 + side) + half) for side in (-1, 1) for half in (0, 1)]
    pair9 = 1 - top // 8
    pairs += [level7(4 * pair9 + quarter) for quarter in range(4)]
    lifted = lift(jnp.concatenate(pairs, 0))
    sides[8] = jnp.concatenate([lifted[:VECS], lifted[VECS : 2 * VECS]], 1)
    other = lift(lifted[2 * VECS :])
    is_upper = (pair9 == 0).astype(F32)
    sides[9] = jnp.concatenate([other * is_upper, other * (1.0 - is_upper)], 1)
    local = None
    for level in (9, 8, 7):
        far = dot3(sides[level], coupling_ref[2 * level - 14], coupling_ref[2 * level - 13])
        if local is not None:
            far = far + dot3(local, *sink)
        is_low = index // (1 << (level - 3)) % 2 == 0
        local = jnp.where(is_low, far[:, :64], far[:, 64:])
    local = local_ref[...] + dot3(local, *split(path_ref[...]))
    far = dot3(local, high_ref[...], low_ref[...])
    out_ref[...] = (base_ref[...] + far) * occ_ref[...]


VMEM = pl.BlockSpec(memory_space=pltpu.VMEM)
SMEM = pl.BlockSpec(memory_space=pltpu.SMEM)
HBM = pl.BlockSpec(memory_space=pltpu.HBM)
ANY = pl.BlockSpec(memory_space=pl.ANY)


def call(body, in_specs, outs, scratch=(), aliases=None, name=None):
    return pl.pallas_call(
        body,
        out_shape=[jax.ShapeDtypeStruct(shape, dtype) for shape, dtype in outs],
        in_specs=in_specs,
        out_specs=[VMEM] * len(outs),
        scratch_shapes=list(scratch),
        input_output_aliases=aliases or {},
        compiler_params=pltpu.CompilerParams(vmem_limit_bytes=VMEM_LIMIT),
        name=name,
    )


def local(points, vectors, counts):
    devices = lax.axis_size(AXES)
    index = lax.axis_index(AXES).astype(jnp.int32)

    def crossed(value, mask):
        return lax.ppermute(value, AXES, [(i, i ^ mask) for i in range(devices)])

    def swapped(value, size):
        pairs = []
        for i in range(size, devices - size):
            pairs.append((i, i + size if i // size % 2 else i - size))
        return lax.ppermute(value, AXES, pairs)

    def after(value, *others):
        return lax.optimization_barrier((value,) + others)[0]

    octants, along = transfer_tables()
    octants = jnp.asarray(hi_lo(octants.T))
    sink = jnp.asarray(hi_lo(along.T))
    layers = jnp.asarray(
        np.concatenate([hi_lo(kernel_table(layer_nodes(0), layer_nodes(z))) for z in (2, 3)])
    )
    couplings = [hi_lo(pair_coupling(level)) for level in range(TOP)]
    low_couplings = jnp.asarray(np.concatenate(couplings[:7]))
    high_couplings = jnp.asarray(np.concatenate(couplings[7:]))

    coords, masked, occupied, box3, far_high, far_low = call(
        head_kernel,
        [SMEM, HBM, HBM, HBM],
        [
            ((8, SLOTS), F32),
            ((VECS, SLOTS), F32),
            ((1, SLOTS), F32),
            ((16, 128), F32),
            ((64, SLOTS), BF16),
            ((64, SLOTS), BF16),
        ],
        [
            pltpu.SMEM((CUBES, 8), jnp.int32),
            pltpu.VMEM((3, SLOTS), F32),
            pltpu.VMEM((VECS, SLOTS), F32),
            pltpu.SemaphoreType.DMA((4,)),
        ],
        name="head",
    )((index * CUBES)[None], counts, points, vectors)

    number = index[None]

    def near_part(part, *holds):
        own = pltpu.VMEM((256, 256), BF16)
        begin, end = part
        width = 256 * (min(end + 1, LAYERS) - begin)
        return call(
            functools.partial(near_kernel, begin, end),
            [VMEM, VMEM] + [ANY] * len(holds),
            [((VECS, width), F32)],
            [own] * 4 + [pltpu.VMEM((256, 48), BF16)],
            name="near",
        )(coords, masked, *holds)[0]

    parts = [(0, 3), (3, 6), (6, 10), (10, 13), (13, 16)]
    arrived = crossed(box3, 1)
    near = [near_part(parts[0], box3)]
    boxes3 = jnp.stack([box3, after(arrived, near[0])])
    arrived = crossed(boxes3, 2)
    coef, leaf_high, leaf_low, pairs, facing, away = call(
        leaf_kernel,
        [SMEM] + [VMEM] * 4 + [ANY],
        [
            ((VECS, SLOTS), F32),
            ((64, SLOTS), BF16),
            ((64, SLOTS), BF16),
            ((7 * VECS, 128), F32),
            ((VECS, 1280), F32),
            ((VECS, 1280), F32),
        ],
        name="leaf",
    )(number, coords, masked, octants, sink, boxes3)
    slots = pltpu.VMEM((4, VECS, 64), F32)
    quad3, close3, wide3 = call(
        lower_gather_kernel,
        [SMEM] + [VMEM] * 3 + [ANY],
        [((VECS, 256), F32), ((144, 128), F32), ((80, 128), F32)],
        [slots],
        name="gather3",
    )(number, boxes3, arrived, sink, pairs)
    others = [crossed(close3, 4), crossed(wide3, 8), crossed(wide3, 12)]
    near.append(near_part(parts[1], wide3))
    quad5, box7, inside, close5, wide5 = call(
        upper_gather_kernel,
        [SMEM] + [VMEM] * 5 + [ANY],
        [
            ((VECS, 256), F32),
            ((16, 128), F32),
            ((128, 128), F32),
            ((144, 128), F32),
            ((128, 128), F32),
        ],
        [slots, pltpu.VMEM((4, 64, 128), F32)],
        name="gather5",
    )(number, wide3, *others, sink, near[-1])
    beside5 = crossed(close5, 16)
    near.append(near_part(parts[2], box7))
    boxes = jnp.stack([box7, after(beside5, near[-1])[:16]])
    arrived = crossed(boxes, 32)
    facing = crossed(after(facing, boxes), 1)
    away = swapped(after(away, boxes), 1)
    near.append(near_part(parts[3], boxes))
    boxes = jnp.concatenate([boxes, after(arrived, near[-1])], 0)
    arrived = crossed(boxes, 64)
    outer5 = swapped(after(wide5, boxes), 16)
    near.append(near_part(parts[4], boxes, facing, away))
    boxes = jnp.concatenate([boxes, after(arrived, near[-1])], 0)
    arrived = crossed(boxes, 128)
    halo = pltpu.VMEM((VECS, 1280), F32)
    base, far_local, path = call(
        functools.partial(rim_kernel, parts),
        [SMEM] + [VMEM] * (17 + len(parts)) + [ANY],
        [((VECS, SLOTS), F32), ((VECS, 64), F32), ((64, 64), F32)],
        [pltpu.VMEM((256, 256), BF16)] * 2 + [halo] * 2,
        name="rim",
    )(
        number, coords, masked, coef, leaf_high, leaf_low, pairs, facing, away, layers,
        low_couplings, sink, octants, quad3, quad5, inside, beside5, outer5, *near, boxes,
    )
    return call(
        tail_kernel,
        [SMEM] + [VMEM] * 10,
        [((VECS, SLOTS), F32)],
        name="tail",
    )(
        number, base, occupied, far_high, far_low, boxes, after(arrived, base), far_local, path,
        high_couplings, sink,
    )[0]


def solution(mesh):
    in_specs = (P(None, AXES), P(None, AXES), P(AXES, None))
    return jax.shard_map(
        local, mesh=mesh, in_specs=in_specs, out_specs=P(None, AXES), check_vma=False
    )
```

```python
import functools
import math

import jax
import jax.numpy as jnp
import ml_dtypes
import numpy as np
from jax import lax
from jax.experimental import pallas as pl
from jax.experimental.pallas import tpu as pltpu
from jax.sharding import PartitionSpec as P

ORDER = 4
VECS = 32
CUBES = 8
LAYERS = 16
SLOTS = 4096
TOP = 10
ROOT_THREE = math.sqrt(3.0)
AXES = ("leaf", "sub")
F32 = jnp.float32
BF16 = jnp.bfloat16
NN = (((1,), (0,)), ((), ()))
NT = (((1,), (1,)), ((), ()))
NODES = np.cos((2.0 * np.arange(ORDER) + 1.0) * np.pi / (2.0 * ORDER))
LENGTHS = [512.0, 64.0, 8.0, 1.0]
STRETCH = ROOT_THREE / math.log(2.0)
VMEM_LIMIT = 16 * 1024 * 1024


def lagrange_table(values):
    columns = []
    for anchor in range(ORDER):
        product = values * 0.0 + 1.0
        for against in range(ORDER):
            if against != anchor:
                product = product * (values - NODES[against]) / (NODES[anchor] - NODES[against])
        columns.append(product)
    return np.stack(columns, -1)


def grid_nodes():
    z, y, x = np.meshgrid(np.arange(ORDER), np.arange(ORDER), np.arange(ORDER), indexing="ij")
    return np.stack([NODES[x.ravel()], NODES[y.ravel()], NODES[z.ravel()]], -1)


def kernel_table(targets, sources):
    gaps = targets[:, None, :] - sources[None, :, :]
    distance = np.sqrt(np.sum(gaps * gaps, -1))
    total = distance * 0.0
    for length in LENGTHS:
        scaled = distance * (ROOT_THREE / length)
        total = total + (1.0 + scaled) * np.exp(-scaled) / (32.0 * math.sqrt(length))
    return total


def layer_nodes(layer):
    scaled = grid_nodes() * 0.25
    leaves = []
    for row in range(2):
        for column in range(2):
            centre = [(column + 0.5) * 0.5, (row + 0.5) * 0.5, (layer + 0.5) * 0.5]
            leaves.append(scaled + np.array(centre))
    return np.concatenate(leaves)


def pair_coupling(level):
    span = float(1 << level)
    nodes = grid_nodes() * np.array([0.5, 0.5, 0.5 * span])

    def block(offset):
        return kernel_table(nodes, nodes + np.array([0.0, 0.0, offset * span])).T

    zero = np.zeros((64, 64))
    before = np.block([[block(-2), block(-3)], [zero, block(-2)]])
    after = np.block([[block(2), zero], [block(3), block(2)]])
    return np.concatenate([before, after], 0)


def transfer_tables():
    halves = [lagrange_table(side + 0.5 * NODES) for side in (-0.5, 0.5)]
    eye = np.eye(ORDER)
    octants = [
        np.kron(np.kron(halves[z], halves[y]), halves[x])
        for z in range(2)
        for y in range(2)
        for x in range(2)
    ]
    along = [np.kron(np.kron(half, eye), eye) for half in halves]
    return np.concatenate(octants, 0), np.concatenate(along, 0)


def hi_lo(table):
    high = table.astype(ml_dtypes.bfloat16)
    low = (table - high.astype(np.float64)).astype(ml_dtypes.bfloat16)
    return np.stack([high, low])


def split(x):
    high = x.astype(BF16)
    return high, (x - high.astype(F32)).astype(BF16)


def mxu(a, b, dims=NN):
    return lax.dot_general(a, b, dims, preferred_element_type=F32)


def dot3(x, high, low, dims=NN):
    rows = x.shape[0]
    x_high, x_low = split(x)
    both = mxu(jnp.concatenate([x_high, x_low], 0), high, dims)
    return both[:rows] + both[rows:] + mxu(x_high, low, dims)


def poly4(u):
    gaps = [u - float(node) for node in NODES]
    polys = []
    for anchor in range(ORDER):
        scale = 1.0
        product = None
        for against in range(ORDER):
            if against != anchor:
                scale = scale / float(NODES[anchor] - NODES[against])
                product = gaps[against] if product is None else product * gaps[against]
        polys.append(product * scale)
    return polys


def basis64(u):
    count = u.shape[1]
    polys = poly4(u)
    row = lax.broadcasted_iota(jnp.int32, (16, count), 0)

    def picked(dim, key):
        rows = [jnp.broadcast_to(poly[dim : dim + 1], (16, count)) for poly in polys]
        low = jnp.where(key == 0, rows[0], rows[1])
        high = jnp.where(key == 2, rows[2], rows[3])
        return jnp.where(key < 2, low, high)

    plane = picked(0, row % 4) * picked(1, row // 4)
    return jnp.concatenate([plane * poly[2:3] for poly in polys], 0)


def stack_rows(x, width):
    return jnp.concatenate(
        [x[:, i * width : (i + 1) * width] for i in range(x.shape[1] // width)], 0
    )


def pair_rows(boxes):
    count = boxes.shape[0] // VECS
    parts = [boxes[i * VECS : (i + 1) * VECS] for i in range(count)]
    return jnp.concatenate(
        [jnp.concatenate(parts[i : i + 2], 1) for i in range(0, count, 2)], 0
    )


def unpair_rows(pairs):
    count = pairs.shape[0] // VECS
    parts = []
    for i in range(count):
        block = pairs[i * VECS : (i + 1) * VECS]
        parts += [block[:, :64], block[:, 64:]]
    return jnp.concatenate(parts, 0)


def pack_box(box):
    return jnp.concatenate([box[:16], box[16:]], 1)


def unpack_box(packed):
    return jnp.concatenate([packed[:, :64], packed[:, 64:]], 0)


def features(coords, origin):
    row = lax.broadcasted_iota(jnp.int32, coords.shape, 0)
    q = (coords - jnp.where(row == 2, origin, 0.0)) * STRETCH
    norm = jnp.sum(q * q, axis=0, keepdims=True)
    left = jnp.where(row == 3, norm, jnp.where(row == 4, 1.0, q))
    right = jnp.where(row == 3, 1.0, jnp.where(row == 4, norm, -2.0 * q))
    return left, right


def three_parts(x):
    first = x.astype(BF16).astype(F32)
    rest = x - first
    second = rest.astype(BF16).astype(F32)
    return first, second, rest - second


def left_side(left):
    f1, f2, f3 = three_parts(left)
    return jnp.concatenate([f1, f1, f2, f2, f1, f3], 0)


def right_side(right):
    g1, g2, g3 = three_parts(right)
    return jnp.concatenate([g1, g2, g1, g2, g3, g1], 0).astype(BF16)


def matern(squared):
    squared = jnp.maximum(squared, 1e-20)
    w = squared * lax.rsqrt(squared)
    total = None
    for length in LENGTHS:
        weight = 1.0 / (32.0 * math.sqrt(length))
        slope = weight * math.log(2.0) / length
        term = (weight + slope * w) * jnp.exp2(w * (-1.0 / length))
        total = term if total is None else total + term
    return total


def fill_weights(turned, sources, high_ref, low_ref, top=0, begin=0):
    rows, columns = turned.shape[0], sources.shape[1]
    step = 128
    for row in range(0, rows, step):
        values = matern(mxu(turned[row : row + step], sources))
        high, low = split(values)
        at = slice(top + row, top + row + step), slice(begin, begin + columns)
        high_ref[at] = high
        low_ref[at] = low


def turned_side(left):
    return jnp.transpose(left_side(left)).astype(BF16)


def head_kernel(slab_ref, counts_hbm, points_hbm, vectors_hbm, coords_ref, masked_ref, occ_ref,
                box_ref, high_ref, low_ref, counts_ref, points_ref, vectors_ref, sems):
    first = slab_ref[0].astype(F32)
    lane = lax.broadcasted_iota(jnp.int32, (1, 512), 1)
    row = lax.broadcasted_iota(jnp.int32, (8, 512), 0)
    copies = [
        pltpu.make_async_copy(counts_hbm, counts_ref, sems.at[0]),
        pltpu.make_async_copy(points_hbm, points_ref, sems.at[1]),
    ]
    half = SLOTS // 2
    for part in range(2):
        at = slice(part * half, part * half + half)
        copies.append(
            pltpu.make_async_copy(vectors_hbm.at[:, at], vectors_ref.at[:, at], sems.at[2 + part])
        )
    for copy in copies:
        copy.start()

    def cube(s, total):
        at = pl.ds(pl.multiple_of(s * 512, 512), 512)
        filled = jnp.zeros((1, 512), jnp.int32)
        for c in range(8):
            filled = jnp.where(lane // 64 == c, counts_ref[s, c], filled)
        occupied = (lane % 64 < filled).astype(F32)
        occ_ref[:, at] = occupied
        masked = vectors_ref[:, at] * occupied
        masked_ref[:, at] = masked
        points = points_ref[:, at]
        points = jnp.concatenate([points, jnp.zeros((5, 512), F32)], 0)
        shift = jnp.where(row == 2, first, jnp.where(row < 2, 0.5, 0.0))
        coords = points - shift
        coords_ref[:, at] = coords
        u = (coords - jnp.where(row == 2, 4.0, 0.0)) * jnp.where(row == 2, 0.25, 2.0)
        high, low = split(basis64(u))
        high_ref[:, at] = high
        low_ref[:, at] = low
        return total + dot3(masked, high, low, NT)

    for copy in copies[:3]:
        copy.wait()
    total = lax.fori_loop(0, CUBES // 2, cube, jnp.zeros((VECS, 64), F32), unroll=2)
    copies[3].wait()
    total = lax.fori_loop(CUBES // 2, CUBES, cube, total, unroll=2)
    box_ref[...] = pack_box(total)


def spread_basis(high, low):
    lane = lax.broadcasted_iota(jnp.int32, (1, 256), 1)
    highs, lows = [], []
    for leaf in range(4):
        mask = (lane // 64 == leaf).astype(F32).astype(BF16)
        highs.append(high * mask)
        lows.append(low * mask)
    return jnp.concatenate(highs, 0), jnp.concatenate(lows, 0)


def leaf_kernel(index_ref, coords_ref, masked_ref, octants_ref, sink_ref, hold_ref, coef_ref,
                high_ref, low_ref, pairs_ref, facing_ref, away_ref):
    del hold_ref
    lane = lax.broadcasted_iota(jnp.int32, (8, 256), 1)
    row = lax.broadcasted_iota(jnp.int32, (8, 256), 0)
    centre_x = jnp.where(lane // 64 % 2 == 0, -0.25, 0.25)
    centre_y = jnp.where(lane // 128 == 0, -0.25, 0.25)

    def layer(z, carry):
        at = pl.ds(pl.multiple_of(z * 256, 256), 256)
        centre_z = z.astype(F32) * 0.5 + 0.25
        centre = jnp.where(row == 0, centre_x, jnp.where(row == 1, centre_y, centre_z))
        u = (coords_ref[:, at] - centre) * 4.0
        high, low = split(basis64(u))
        high_ref[:, at] = high
        low_ref[:, at] = low
        wide_high, wide_low = spread_basis(high, low)
        coef_ref[:, at] = dot3(masked_ref[:, at], wide_high, wide_low, NT)
        return carry

    lax.fori_loop(0, LAYERS, layer, 0, unroll=4)
    boxes = dot3(stack_rows(coef_ref[...], 512), octants_ref[0], octants_ref[1], NT)
    p0 = pair_rows(boxes)
    p1 = pair_rows(dot3(p0, sink_ref[0], sink_ref[1], NT))
    p2 = pair_rows(dot3(p1, sink_ref[0], sink_ref[1], NT))
    pairs_ref[...] = jnp.concatenate([p0, p1, p2], 0)

    def bundle(ref, near, far, low_pair, mid_pair):
        ref[:, 0:256] = masked_ref[:, near : near + 256]
        ref[:, 256:768] = coef_ref[:, far : far + 512]
        ref[:, 768:896] = low_pair
        ref[:, 896:1024] = mid_pair
        ref[:, 1024:1152] = p2
        ref[:, 1152:1280] = jnp.zeros((VECS, 128), F32)
        ref[0:8, 1152:1280] = coords_ref[:, near : near + 128]
        ref[8:16, 1152:1280] = coords_ref[:, near + 128 : near + 256]

    is_even = index_ref[0] % 2 == 0

    @pl.when(is_even)
    def _():
        bundle(facing_ref, SLOTS - 256, SLOTS - 512, p0[96:], p1[32:])
        bundle(away_ref, 0, 0, p0[:32], p1[:32])

    @pl.when(jnp.logical_not(is_even))
    def _():
        bundle(away_ref, SLOTS - 256, SLOTS - 512, p0[96:], p1[32:])
        bundle(facing_ref, 0, 0, p0[:32], p1[:32])


def near_kernel(begin, end, coords_ref, masked_ref, *refs):
    near_ref, own_high, own_low, next_high, next_low, turned_ref = refs[-6:]
    near_ref[...] = jnp.zeros_like(near_ref)

    def out(z):
        return pl.ds(pl.multiple_of((z - begin) * 256, 256), 256)

    def lanes(z):
        return pl.ds(pl.multiple_of(z * 256, 256), 256)

    def top_of(z):
        return jnp.asarray(z, F32) * 0.5 + 0.5

    def fill_own(z):
        left, right = features(coords_ref[:, lanes(z)], top_of(z))
        turned = turned_side(left)
        turned_ref[...] = turned
        sources = right_side(right)
        fill_weights(turned[:128], sources, own_high, own_low)
        fill_weights(turned[128:], sources[:, 128:], own_high, own_low, 128, 128)

    def fill_next(z):
        _, right = features(coords_ref[:, lanes(z + 1)], top_of(z))
        fill_weights(turned_ref[...], right_side(right), next_high, next_low)

    def add_own(z):
        x = masked_ref[:, lanes(z)]
        both = dot3(x[:, :128], own_high[:128], own_low[:128])
        first = dot3(x[:, 128:], own_high[:128, 128:], own_low[:128, 128:], NT)
        second = dot3(x[:, 128:], own_high[128:, 128:], own_low[128:, 128:])
        near_ref[:, out(z)] += both + jnp.concatenate([first, second], 1)

    def add_next(z):
        near_ref[:, out(z)] += dot3(masked_ref[:, lanes(z + 1)], next_high[...], next_low[...], NT)
        near_ref[:, out(z + 1)] += dot3(masked_ref[:, lanes(z)], next_high[...], next_low[...])

    def layer(z, carry):
        fill_next(z)
        add_own(z)
        fill_own(z + 1)
        add_next(z)
        return carry

    fill_own(begin)
    lax.fori_loop(begin, end - 1, layer, 0)
    if end < LAYERS:
        fill_next(end - 1)
    add_own(end - 1)
    if end < LAYERS:
        add_next(end - 1)


def four_to_one(slots, sink_ref):
    left = jnp.concatenate([slots[0], slots[1]], 1)
    right = jnp.concatenate([slots[2], slots[3]], 1)
    lifted = dot3(jnp.concatenate([left, right], 0), sink_ref[0], sink_ref[1], NT)
    pair = pair_rows(lifted)
    box = pack_box(dot3(pair, sink_ref[0], sink_ref[1], NT))
    return left, right, pair, box


def lower_gather_kernel(index_ref, own_ref, far_ref, sink_ref, hold_ref, quad_ref, close_ref,
                        wide_ref, slots):
    del hold_ref
    index = index_ref[0]
    for step, box in enumerate((own_ref[0], own_ref[1], far_ref[0], far_ref[1])):
        slots[pl.ds(index % 4 ^ step, 1)] = unpack_box(box)[None]
    left, right, pair, box = four_to_one(slots, sink_ref)
    quad_ref[...] = jnp.concatenate([left, right], 1)
    is_even = index // 4 % 2 == 0
    facing = jnp.where(is_even, right, left)
    away = jnp.where(is_even, left, right)
    close_ref[...] = jnp.concatenate([box, facing, pair, away, pair], 0)
    wide_ref[...] = jnp.concatenate([box, away, pair], 0)


def upper_gather_kernel(index_ref, own_ref, one_ref, two_ref, three_ref, sink_ref, hold_ref,
                        quad_ref, box_ref, inside_ref, close_ref, wide_ref, slots, edges):
    del hold_ref
    index = index_ref[0]
    member = index // 4 % 4
    for step, ref in enumerate((own_ref, one_ref, two_ref, three_ref)):
        slots[pl.ds(member ^ step, 1)] = unpack_box(ref[:16])[None]
        edges[pl.ds(member ^ step, 1)] = ref[80:144][None] if step == 1 else ref[16:80][None]
    left, right, pair, box = four_to_one(slots, sink_ref)
    quad_ref[...] = jnp.concatenate([left, right], 1)
    box_ref[...] = box
    beside, across = one_ref[16:80], three_ref[16:80]
    is_odd = member % 2 == 1
    inside_ref[:64] = jnp.where(is_odd, beside, across)
    inside_ref[64:] = jnp.where(is_odd, across, beside)
    is_even = index // 16 % 2 == 0
    first, last = edges[0], edges[3]
    facing = jnp.where(is_even, right, left)
    away = jnp.where(is_even, left, right)
    close_ref[...] = jnp.concatenate([box, facing, pair, jnp.where(is_even, last, first)], 0)
    wide_ref[...] = jnp.concatenate([away, pair, jnp.where(is_even, first, last)], 0)


def rim_kernel(parts, index_ref, coords_ref, masked_ref, coef_ref, basish_ref, basisl_ref,
               pairs_ref, facing_ref, away_ref, layers_ref, coupling_ref, sink_ref, octants_ref,
               quad3_ref, quad5_ref, inside_ref, close_ref, wide_ref, *refs):
    near_refs = refs[: len(parts)]
    _, base_ref, local_ref, path_ref, high_ref, low_ref, left_ref, right_ref = refs[len(parts) :]
    index = index_ref[0]
    base_ref[...] = jnp.zeros_like(base_ref)
    for (begin, end), ref in zip(parts, near_refs):
        base_ref[:, 256 * begin : min(256 * end + 256, SLOTS)] += ref[...]
    is_even = index % 2 == 0
    left_ref[...] = jnp.where(is_even, away_ref[...], facing_ref[...])
    right_ref[...] = jnp.where(is_even, facing_ref[...], away_ref[...])
    row = lax.broadcasted_iota(jnp.int32, (8, 256), 0)

    def rim_coords(ref, shift):
        coords = jnp.concatenate([ref[0:8, 1152:1280], ref[8:16, 1152:1280]], 1)
        return coords + jnp.where(row == 2, shift, 0.0)

    low_rim = rim_coords(left_ref, -float(CUBES))
    left, _ = features(low_rim, 0.0)
    _, right = features(coords_ref[:, :256], 0.0)
    fill_weights(turned_side(left), right_side(right), high_ref, low_ref)
    base_ref[:, :256] += dot3(left_ref[:, :256], high_ref[...], low_ref[...], NN)
    high_rim = rim_coords(right_ref, float(CUBES))
    left, _ = features(coords_ref[:, SLOTS - 256 :], float(CUBES))
    _, right = features(high_rim, float(CUBES))
    fill_weights(turned_side(left), right_side(right), high_ref, low_ref)
    base_ref[:, SLOTS - 256 :] += dot3(right_ref[:, :256], high_ref[...], low_ref[...], NT)

    coefs = [coef_ref[:, 512 * s : 512 * s + 512] for s in range(CUBES)]
    before = jnp.concatenate([left_ref[:, 256:768]] + coefs[:-1], 0)
    after = jnp.concatenate(coefs[1:] + [right_ref[:, 256:768]], 0)
    k2 = (layers_ref[0], layers_ref[1])
    k3 = (layers_ref[2], layers_ref[3])
    even = dot3(before[:, :256], *k2) + dot3(after[:, :256], *k2, NT) + dot3(after[:, 256:], *k3, NT)
    odd = dot3(before[:, :256], *k3) + dot3(before[:, 256:], *k2) + dot3(after[:, 256:], *k2, NT)

    def coupled(pairs, level):
        at = slice(768 + 128 * level, 896 + 128 * level)
        lower, upper = left_ref[:, at], right_ref[:, at]
        sides = jnp.concatenate(
            [
                jnp.concatenate([lower, pairs[:-VECS]], 0) if pairs.shape[0] > VECS else lower,
                jnp.concatenate([pairs[VECS:], upper], 0) if pairs.shape[0] > VECS else upper,
            ],
            1,
        )
        return dot3(sides, coupling_ref[2 * level], coupling_ref[2 * level + 1])

    sink = (sink_ref[0], sink_ref[1])
    local = coupled(pairs_ref[6 * VECS :], 2)
    local = coupled(pairs_ref[4 * VECS : 6 * VECS], 1) + dot3(unpair_rows(local), *sink)
    local = coupled(pairs_ref[: 4 * VECS], 0) + dot3(unpair_rows(local), *sink)
    inherited = dot3(unpair_rows(local), octants_ref[0], octants_ref[1])
    even = even + inherited[:, :256]
    odd = odd + inherited[:, 256:]
    for s in range(CUBES):
        for part, values in ((0, even), (1, odd)):
            at = slice(512 * s + 256 * part, 512 * s + 256 * part + 256)
            high, low = spread_basis(basish_ref[:, at], basisl_ref[:, at])
            base_ref[:, at] += dot3(values[VECS * s : VECS * s + VECS], high, low)

    member = index // 4 % 4
    is_even = index // 16 % 2 == 0
    beside, outer = close_ref[...], wide_ref[...]
    left = jnp.where(member == 0, jnp.where(is_even, outer[64:], beside[80:]), inside_ref[:64])
    right = jnp.where(member == 3, jnp.where(is_even, beside[80:], outer[64:]), inside_ref[64:])
    edges = {
        3: (left, right),
        5: (
            jnp.where(is_even, outer[:64], beside[16:80]),
            jnp.where(is_even, beside[16:80], outer[:64]),
        ),
    }

    def is_low(level):
        return index // (1 << (level - 3)) % 2 == 0

    def half(both, level):
        return jnp.where(is_low(level), both[:, :64], both[:, 64:])

    sides = {}
    for level, quad_ref in ((3, quad3_ref), (5, quad5_ref)):
        left, right = edges[level]
        low = is_low(level + 1)
        sides[level] = jnp.concatenate(
            [
                jnp.where(low, left[:VECS], quad_ref[:, :128]),
                jnp.where(low, quad_ref[:, 128:], right[:VECS]),
            ],
            1,
        )
        sides[level + 1] = jnp.concatenate([left[VECS:], right[VECS:]], 1)
    local = path = None
    for level in (6, 5, 4, 3):
        far = dot3(sides[level], coupling_ref[2 * level], coupling_ref[2 * level + 1])
        step = sink[0].astype(F32) + sink[1].astype(F32)
        if local is not None:
            far = far + dot3(local, *sink)
            step = dot3(path, *sink)
        local = half(far, level)
        path = half(step, level)
    local_ref[...] = local
    path_ref[...] = path


def tail_kernel(index_ref, base_ref, occ_ref, high_ref, low_ref, boxes_ref,
                far_ref, local_ref, path_ref, coupling_ref, sink_ref, out_ref):
    index = index_ref[0]
    top = index // 16
    count = boxes_ref.shape[0]

    def box7(number):
        inside = ((number >= 0) & (number < 16)).astype(F32)
        place = jnp.clip(number, 0, 15) ^ top
        at = pl.ds(place % count, 1)
        packed = jnp.where(place < count, boxes_ref[at][0], far_ref[at][0])
        return unpack_box(packed) * inside

    sink = (sink_ref[0], sink_ref[1])

    def lift(pairs):
        return pair_rows(dot3(pairs, *sink, NT))

    def level7(pair):
        return jnp.concatenate([box7(2 * pair), box7(2 * pair + 1)], 1)

    sides = {}
    pair7 = top // 2
    sides[7] = jnp.concatenate([level7(pair7 - 1), level7(pair7 + 1)], 1)
    pair8 = top // 4
    pairs = [level7(2 * (pair8 + side) + half) for side in (-1, 1) for half in (0, 1)]
    pair9 = 1 - top // 8
    pairs += [level7(4 * pair9 + quarter) for quarter in range(4)]
    lifted = lift(jnp.concatenate(pairs, 0))
    sides[8] = jnp.concatenate([lifted[:VECS], lifted[VECS : 2 * VECS]], 1)
    other = lift(lifted[2 * VECS :])
    is_upper = (pair9 == 0).astype(F32)
    sides[9] = jnp.concatenate([other * is_upper, other * (1.0 - is_upper)], 1)
    local = None
    for level in (9, 8, 7):
        far = dot3(sides[level], coupling_ref[2 * level - 14], coupling_ref[2 * level - 13])
        if local is not None:
            far = far + dot3(local, *sink)
        is_low = index // (1 << (level - 3)) % 2 == 0
        local = jnp.where(is_low, far[:, :64], far[:, 64:])
    local = local_ref[...] + dot3(local, *split(path_ref[...]))
    far = dot3(local, high_ref[...], low_ref[...])
    out_ref[...] = (base_ref[...] + far) * occ_ref[...]


VMEM = pl.BlockSpec(memory_space=pltpu.VMEM)
SMEM = pl.BlockSpec(memory_space=pltpu.SMEM)
HBM = pl.BlockSpec(memory_space=pltpu.HBM)
ANY = pl.BlockSpec(memory_space=pl.ANY)


def call(body, in_specs, outs, scratch=(), aliases=None, name=None):
    return pl.pallas_call(
        body,
        out_shape=[jax.ShapeDtypeStruct(shape, dtype) for shape, dtype in outs],
        in_specs=in_specs,
        out_specs=[VMEM] * len(outs),
        scratch_shapes=list(scratch),
        input_output_aliases=aliases or {},
        compiler_params=pltpu.CompilerParams(vmem_limit_bytes=VMEM_LIMIT),
        name=name,
    )


def local(points, vectors, counts):
    devices = lax.axis_size(AXES)
    index = lax.axis_index(AXES).astype(jnp.int32)

    def crossed(value, mask):
        return lax.ppermute(value, AXES, [(i, i ^ mask) for i in range(devices)])

    def swapped(value, size):
        pairs = []
        for i in range(size, devices - size):
            pairs.append((i, i + size if i // size % 2 else i - size))
        return lax.ppermute(value, AXES, pairs)

    def after(value, *others):
        return lax.optimization_barrier((value,) + others)[0]

    octants, along = transfer_tables()
    octants = jnp.asarray(hi_lo(octants.T))
    sink = jnp.asarray(hi_lo(along.T))
    layers = jnp.asarray(
        np.concatenate([hi_lo(kernel_table(layer_nodes(0), layer_nodes(z))) for z in (2, 3)])
    )
    couplings = [hi_lo(pair_coupling(level)) for level in range(TOP)]
    low_couplings = jnp.asarray(np.concatenate(couplings[:7]))
    high_couplings = jnp.asarray(np.concatenate(couplings[7:]))

    coords, masked, occupied, box3, far_high, far_low = call(
        head_kernel,
        [SMEM, HBM, HBM, HBM],
        [
            ((8, SLOTS), F32),
            ((VECS, SLOTS), F32),
            ((1, SLOTS), F32),
            ((16, 128), F32),
            ((64, SLOTS), BF16),
            ((64, SLOTS), BF16),
        ],
        [
            pltpu.SMEM((CUBES, 8), jnp.int32),
            pltpu.VMEM((3, SLOTS), F32),
            pltpu.VMEM((VECS, SLOTS), F32),
            pltpu.SemaphoreType.DMA((4,)),
        ],
        name="head",
    )((index * CUBES)[None], counts, points, vectors)

    number = index[None]

    def near_part(part, *holds):
        own = pltpu.VMEM((256, 256), BF16)
        begin, end = part
        width = 256 * (min(end + 1, LAYERS) - begin)
        return call(
            functools.partial(near_kernel, begin, end),
            [VMEM, VMEM] + [ANY] * len(holds),
            [((VECS, width), F32)],
            [own] * 4 + [pltpu.VMEM((256, 48), BF16)],
            name="near",
        )(coords, masked, *holds)[0]

    parts = [(0, 4), (4, 7), (7, 11), (11, 14), (14, 16)]
    arrived = crossed(box3, 1)
    near = [near_part(parts[0], box3)]
    boxes3 = jnp.stack([box3, after(arrived, near[0])])
    arrived = crossed(boxes3, 2)
    coef, leaf_high, leaf_low, pairs, facing, away = call(
        leaf_kernel,
        [SMEM] + [VMEM] * 4 + [ANY],
        [
            ((VECS, SLOTS), F32),
            ((64, SLOTS), BF16),
            ((64, SLOTS), BF16),
            ((7 * VECS, 128), F32),
            ((VECS, 1280), F32),
            ((VECS, 1280), F32),
        ],
        name="leaf",
    )(number, coords, masked, octants, sink, boxes3)
    slots = pltpu.VMEM((4, VECS, 64), F32)
    quad3, close3, wide3 = call(
        lower_gather_kernel,
        [SMEM] + [VMEM] * 3 + [ANY],
        [((VECS, 256), F32), ((144, 128), F32), ((80, 128), F32)],
        [slots],
        name="gather3",
    )(number, boxes3, arrived, sink, pairs)
    others = [crossed(close3, 4), crossed(wide3, 8), crossed(wide3, 12)]
    near.append(near_part(parts[1], wide3))
    quad5, box7, inside, close5, wide5 = call(
        upper_gather_kernel,
        [SMEM] + [VMEM] * 5 + [ANY],
        [
            ((VECS, 256), F32),
            ((16, 128), F32),
            ((128, 128), F32),
            ((144, 128), F32),
            ((128, 128), F32),
        ],
        [slots, pltpu.VMEM((4, 64, 128), F32)],
        name="gather5",
    )(number, wide3, *others, sink, near[-1])
    beside5 = crossed(close5, 16)
    near.append(near_part(parts[2], box7))
    boxes = jnp.stack([box7, after(beside5, near[-1])[:16]])
    arrived = crossed(boxes, 32)
    facing = crossed(after(facing, boxes), 1)
    away = swapped(after(away, boxes), 1)
    near.append(near_part(parts[3], boxes))
    boxes = jnp.concatenate([boxes, after(arrived, near[-1])], 0)
    arrived = crossed(boxes, 64)
    outer5 = swapped(after(wide5, boxes), 16)
    near.append(near_part(parts[4], boxes, facing, away))
    boxes = jnp.concatenate([boxes, after(arrived, near[-1])], 0)
    arrived = crossed(boxes, 128)
    halo = pltpu.VMEM((VECS, 1280), F32)
    base, far_local, path = call(
        functools.partial(rim_kernel, parts),
        [SMEM] + [VMEM] * (17 + len(parts)) + [ANY],
        [((VECS, SLOTS), F32), ((VECS, 64), F32), ((64, 64), F32)],
        [pltpu.VMEM((256, 256), BF16)] * 2 + [halo] * 2,
        name="rim",
    )(
        number, coords, masked, coef, leaf_high, leaf_low, pairs, facing, away, layers,
        low_couplings, sink, octants, quad3, quad5, inside, beside5, outer5, *near, boxes,
    )
    return call(
        tail_kernel,
        [SMEM] + [VMEM] * 10,
        [((VECS, SLOTS), F32)],
        name="tail",
    )(
        number, base, occupied, far_high, far_low, boxes, after(arrived, base), far_local, path,
        high_couplings, sink,
    )[0]


def solution(mesh):
    in_specs = (P(None, AXES), P(None, AXES), P(AXES, None))
    return jax.shard_map(
        local, mesh=mesh, in_specs=in_specs, out_specs=P(None, AXES), check_vma=False
    )
```
